256 devices in a mesh: ctx: 128 (over z, y_lo, x, core), tp: 2 (over y_hi).
Axes of the slice: x: 4, y: 4 (y_hi: 2, y_lo: 2; y = y_hi * 2 + y_lo), z: 8, core: 2. Of those that a mesh axis runs over, the one named last changes fastest.
Arguments:
- frames: bfloat16 [16384, 1536], P('ctx'), may hold values from -24 to 24
- norm_gain: float32 [1536], replicated, may hold values from 0.5 to 1.5
- norm_bias: float32 [1536], replicated, may hold values from -3 to 3
- w_glu: bfloat16 [1536, 2, 1536], P(None, None, 'tp'), may hold values from -0.15625 to 0.15625
- kernel: float32 [31, 1536], P(None, 'tp'), may hold values from -1 to 1
- dw_bias: float32 [1536], P('tp'), may hold values from -3 to 3
- w_out: bfloat16 [1536, 1536], P(None, 'tp'), may hold values from -0.15625 to 0.15625
- utt_ends: int32 [4], replicated, may hold values from 1 to 16384, as said below
- valid_frames: int32 [4], replicated, may hold values from 1 to 12288, as said below
- cotangent: bfloat16 [16384, 1536], P('ctx'), may hold values from -24 to 24
Outputs:
- mixed: bfloat16 [16384, 1536], P('ctx')
- grad_frames: bfloat16 [16384, 1536], P('ctx')
- grad_glu: float32 [1536, 2, 1536], P('ctx', None, 'tp')
- grad_out: float32 [1536, 1536], P('ctx', 'tp')
The draws below stay inside these ranges and needn't reach their ends.
Inputs may be any that keep to these rules, and one draw needn't show every extreme that they name: utt_ends rises strictly and its last entry is 16384; the last utterance's slot is the last three quarters of the span, from frame 16384 // 4 on, the others share the first quarter. valid_frames[u] lies between half (rounded up) and all of the frames of utterance u's slot; the remaining frames of the slot are padding; the last utterance has no padding.
All inputs are finite; a program needn't handle non-finite values.
Results may differ from the reference program's by a relative error of at most 0.008.
Values may be sent and summed in bfloat16 or wider, within the bound.
No kernel may reach another device: no remote copies, remote signals or barrier semaphores. Data moves between devices by JAX's collectives and lax.ppermute only.
A program may use at most 128 MiB of HBM per device.

```python
import jax
import jax.numpy as jnp
from jax import lax

D = 1536
KERNEL = 31
UTT = 4
LENGTH = 16384


def utterance_ends(key):
    weights = jax.random.randint(jax.random.fold_in(key, 7), (UTT - 1,), 1, 4)
    running = jnp.cumsum(weights)
    first_part = LENGTH // 4
    leading = first_part * running // running[-1]
    return jnp.concatenate([leading, jnp.full((1,), LENGTH, jnp.int32)]).astype(jnp.int32)


def draw_utt_ends(key, part):
    return utterance_ends(key)


def draw_valid_frames(key, part):
    utt_bounds = utterance_ends(key)
    slot_sizes = utt_bounds - jnp.concatenate([jnp.zeros((1,), jnp.int32), utt_bounds[:-1]])
    padding = jax.random.randint(jax.random.fold_in(key, 11), (UTT,), 0, slot_sizes // 2 + 1)
    is_last = jnp.arange(UTT, dtype=jnp.int32) == UTT - 1
    padding = jnp.where(is_last, 0, padding)
    return (slot_sizes - padding).astype(jnp.int32)


def strengthened(result, rng, source, target, blocks, factor):
    def block_of(axis_at):
        return (jnp.arange(result.shape[axis_at]) // (result.shape[axis_at] // blocks)).reshape((-1,) + (1,) * (result.ndim - 1 - axis_at))

    near = jax.random.permutation(rng, blocks)[block_of(target)]
    second = (block_of(target) + blocks // 2) % blocks
    return jnp.where((block_of(source) == near) | (block_of(source) == second), factor * result, result)


def block_scale(stream_key, dims, split, low, high):
    gain, own = 1.0, jax.random.fold_in(stream_key, 6)
    for axis_at, shards_of in split:
        draws = jnp.exp(jax.random.uniform(jax.random.fold_in(own, axis_at), (shards_of,), jnp.float32, low / len(split), high / len(split)))
        gain = gain * jnp.repeat(draws, dims[axis_at] // shards_of).reshape([-1 if axis == axis_at else 1 for axis in range(len(dims))])
    return gain


def bell_draw(key, dims, width, reach, cuts=(), kind=jnp.bfloat16):
    result = width * jax.random.normal(key, dims, jnp.float32)
    if cuts:
        result = result * block_scale(key, dims, cuts, -0.22, 0.18)
    return jnp.clip(result, -reach, reach).astype(kind)


def heavy_noise(key, shape, deviation, bound, split, heavy, kind=jnp.bfloat16):
    array = deviation * jax.random.normal(key, shape, jnp.float32)
    if split:
        array = array * block_scale(key, shape, split, -0.22, 0.18)
    return jnp.clip(strengthened(array, jax.random.fold_in(key, 3), *heavy), -bound, bound).astype(kind)


def setup_inputs(seed: int = 0) -> dict:
    key_list = jax.random.split(jax.random.key(seed), 11)
    return {
        "frames": heavy_noise(key_list[0], (LENGTH, D), 1.0, 24.0, ((0, 128),), (0, 1, 128, 5.5)),
        "norm_gain": jnp.clip(1.0 + 0.1 * jax.random.normal(key_list[1], (D,), jnp.float32), 0.5, 1.5),
        "norm_bias": bell_draw(key_list[2], (D,), 0.5, 3.0, (), jnp.float32),
        "w_glu": bell_draw(key_list[3], (D, 2, D), D ** -0.5, 0.15625, ((2, 2),)),
        "kernel": bell_draw(key_list[4], (KERNEL, D), KERNEL ** -0.5, 1.0, ((1, 2),), jnp.float32),
        "dw_bias": bell_draw(key_list[5], (D,), 0.5, 3.0, ((0, 2),), jnp.float32),
        "w_out": bell_draw(key_list[6], (D, D), D ** -0.5, 0.15625, ((1, 2),)),
        "utt_ends": draw_utt_ends(jax.random.fold_in(key_list[10], 71), 0),
        "valid_frames": draw_valid_frames(jax.random.fold_in(key_list[10], 71), 0),
        "cotangent": heavy_noise(key_list[9], (LENGTH, D), 1.0, 24.0, ((0, 128),), (0, 1, 128, 5.5)),
    }


norm_epsilon = 1e-05

def frame_info(utt_ends, valid_frames, positions):
    seg_index = lax.optimization_barrier(jnp.sum((positions[:, None] >= utt_ends[None, :]).astype(jnp.int32), axis=1))
    prior_ends = jnp.concatenate([jnp.zeros((1,), jnp.int32), utt_ends[:-1]])
    chosen = seg_index[:, None] == jnp.arange(utt_ends.shape[0], dtype=jnp.int32)[None, :]
    seg_start = lax.optimization_barrier(jnp.sum(jnp.where(chosen, prior_ends[None, :], 0), axis=1))
    seg_valid = lax.optimization_barrier(jnp.sum(jnp.where(chosen, valid_frames[None, :], 0), axis=1))
    inside = (positions - seg_start < seg_valid).astype(jnp.float32)
    return (seg_index, inside)

def depthwise(padded, kernel, seg_window, half_taps, row_count):
    seg_own = seg_window[half_taps:half_taps + row_count]
    summed = jnp.zeros((row_count, padded.shape[1]), jnp.float32)
    for tap_index in range(kernel.shape[0]):
        same_seg = (seg_window[tap_index:tap_index + row_count] == seg_own).astype(jnp.float32)[:, None]
        summed = summed + kernel[tap_index] * (padded[tap_index:tap_index + row_count].astype(jnp.float32) * same_seg)
    return summed

def depthwise_back(padded, kernel, seg_window, half_taps, row_count):
    seg_own = seg_window[half_taps:half_taps + row_count]
    summed = jnp.zeros((row_count, padded.shape[1]), jnp.float32)
    for tap_index in range(kernel.shape[0]):
        shift = 2 * half_taps - tap_index
        same_seg = (seg_window[shift:shift + row_count] == seg_own).astype(jnp.float32)[:, None]
        summed = summed + kernel[tap_index] * (padded[shift:shift + row_count].astype(jnp.float32) * same_seg)
    return summed

def reference(frames, norm_gain, norm_bias, w_glu, kernel, dw_bias, w_out, utt_ends, valid_frames, cotangent):
    half_taps = KERNEL // 2
    positions = jnp.arange(-half_taps, LENGTH + half_taps, dtype=jnp.int32)
    seg_window, valid_window = frame_info(utt_ends, valid_frames, positions)
    valid_mask = valid_window[half_taps:half_taps + LENGTH][:, None]
    source = frames.astype(jnp.float32)
    average = lax.optimization_barrier(jnp.mean(source, axis=1, keepdims=True))
    centred = source - average
    variance = lax.optimization_barrier(jnp.mean(centred * centred, axis=1, keepdims=True))
    inv_std = lax.rsqrt(variance + norm_epsilon)
    standard = centred * inv_std
    normed = (standard * norm_gain + norm_bias).astype(jnp.bfloat16)
    w_flat = w_glu.reshape(D, 2 * D)
    pre_act = jnp.dot(normed, w_flat, preferred_element_type=jnp.float32).reshape(LENGTH, 2, D)
    value_part = pre_act[:, 0, :]
    gate_part = pre_act[:, 1, :]
    gate_sig = jax.nn.sigmoid(gate_part)
    glu_out = (valid_mask * value_part * gate_sig).astype(jnp.bfloat16)
    padded = jnp.pad(glu_out, ((half_taps, half_taps), (0, 0)))
    conv_out = depthwise(padded, kernel, seg_window, half_taps, LENGTH) + dw_bias
    conv_sig = jax.nn.sigmoid(conv_out)
    activation = (conv_out * conv_sig).astype(jnp.bfloat16)
    branch = jnp.dot(activation, w_out.T, preferred_element_type=jnp.float32)
    mixed = (source + valid_mask * branch).astype(jnp.bfloat16)
    masked_grad = (valid_mask * cotangent.astype(jnp.float32)).astype(jnp.bfloat16)
    grad_scale = float(LENGTH) ** (-0.5)
    grad_out = jnp.dot(masked_grad.T, activation, preferred_element_type=jnp.float32) * grad_scale
    grad_act = jnp.dot(masked_grad, w_out, preferred_element_type=jnp.float32)
    grad_conv = (grad_act * conv_sig * (1.0 + conv_out * (1.0 - conv_sig))).astype(jnp.bfloat16)
    grad_padded = jnp.pad(grad_conv, ((half_taps, half_taps), (0, 0)))
    grad_glu_out = depthwise_back(grad_padded, kernel, seg_window, half_taps, LENGTH)
    grad_value = valid_mask * grad_glu_out * gate_sig
    grad_gate = valid_mask * grad_glu_out * value_part * gate_sig * (1.0 - gate_sig)
    grad_pre = jnp.stack([grad_value, grad_gate], axis=1).astype(jnp.bfloat16).reshape(LENGTH, 2 * D)
    grad_glu = (jnp.dot(normed.T, grad_pre, preferred_element_type=jnp.float32) * grad_scale).reshape(D, 2, D)
    grad_normed = jnp.dot(grad_pre, w_flat.T, preferred_element_type=jnp.float32)
    scaled = grad_normed * norm_gain
    first_mean = lax.optimization_barrier(jnp.mean(scaled, axis=1, keepdims=True))
    second_mean = lax.optimization_barrier(jnp.mean(scaled * standard, axis=1, keepdims=True))
    grad_frames = (cotangent.astype(jnp.float32) + inv_std * (scaled - first_mean - standard * second_mean)).astype(jnp.bfloat16)
    return (mixed, grad_frames, grad_glu, grad_out)
```

```python
import functools

import jax
import jax.numpy as jnp
from jax import lax
from jax.experimental import pallas as pl
from jax.experimental.pallas import tpu as pltpu
from jax.sharding import PartitionSpec as P

EPS = 1e-05
HALF = 15
F32 = jnp.float32
BF16 = jnp.bfloat16
VM = pltpu.VMEM
SM = pltpu.SMEM


def params(mib=48):
    return pltpu.CompilerParams(vmem_limit_bytes=mib * 1024 * 1024)


def call(kernel, out_shape, in_spaces, scratch=(), mib=48, cost=None):
    return pl.pallas_call(
        kernel,
        out_shape=out_shape,
        in_specs=[pl.BlockSpec(memory_space=s) for s in in_spaces],
        out_specs=jax.tree.map(lambda _: pl.BlockSpec(memory_space=VM), out_shape),
        scratch_shapes=list(scratch),
        compiler_params=params(mib),
        cost_estimate=cost,
    )


def shape(dims, kind):
    return jax.ShapeDtypeStruct(dims, kind)


def frame_info(ends_ref, real_ref, start, rows, length):
    count = ends_ref.shape[0]
    pos = start + lax.broadcasted_iota(jnp.int32, (rows, 128), 0)
    seg = jnp.zeros((rows, 128), jnp.int32)
    limit = jnp.zeros((rows, 128), jnp.int32) + real_ref[0]
    for u in range(count):
        past = pos >= ends_ref[u]
        seg = seg + past.astype(jnp.int32)
        after = ends_ref[u] + real_ref[u + 1] if u + 1 < count else 0
        limit = jnp.where(past, after, limit)
    inside = (pos >= 0) & (pos < length) & (pos < limit)
    return seg, inside.astype(F32)


def wide(mask, columns):
    return jnp.concatenate([mask] * (columns // 128), axis=1)


def standard(rows):
    source = rows.astype(F32)
    centred = source - jnp.mean(source, axis=1, keepdims=True)
    variance = jnp.mean(centred * centred, axis=1, keepdims=True)
    inv_std = lax.rsqrt(variance + EPS)
    return centred * inv_std, inv_std


def dot_cols(left, right):
    return lax.dot_general(left, right, (((1,), (1,)), ((), ())), preferred_element_type=F32)


def norm_kernel(
    length, where, ends, real, frames, cot, gain, bias, normed, t0, t1, t2, t3, tall, picked
):
    xhat, _ = standard(frames[...])
    own = (xhat * gain[...] + bias[...]).astype(BF16)
    normed[...] = own
    rows = frames.shape[0]
    _, valid = frame_info(ends, real, where[0], rows, length)
    masked = wide(valid, frames.shape[1]) * cot[...].astype(F32)
    x = where[1]
    for n, values in enumerate((own.astype(F32), masked)):
        tall[...] = values.T
        for k, out in enumerate((t0, t1, t2, t3)):
            at = lax.rem(x + k, 4) * 24
            for zy in range(16):
                picked[pl.ds(zy * 24, 24), :] = tall[pl.ds(pl.multiple_of(zy * 96 + at, 8), 24), :]
            out[n] = picked[...].astype(BF16)


def taps(source, seg_source, seg_own, kernel, first_of, start, rows, columns):
    groups = columns // 128
    sums = [jnp.zeros((rows, 128), F32) for _ in range(groups)]
    for k in range(2 * HALF + 1):
        at = start + first_of(k)
        same = seg_source[pl.ds(at, rows), :] == seg_own
        for g in range(groups):
            lanes = pl.ds(g * 128, 128)
            piece = jnp.where(same, source[pl.ds(at, rows), lanes], 0.0)
            sums[g] = sums[g] + kernel[pl.ds(k, 1), lanes] * piece
    return sums


def forward_kernel(
    length, where, ends, real, normed, prior, following, gain, bias, w2, kernel, dw_bias, w_out,
    value, gate, conv, act_keep, act_send, mixed, normed_all, glu, seg_all, act_all,
):
    rows, hidden = normed.shape[0], w_out.shape[1]
    for part, at in ((prior, 0), (following, rows + 32)):
        xhat, _ = standard(part[pl.ds(0, 32), :])
        normed_all[pl.ds(at, 32), :] = (xhat * gain[...] + bias[...]).astype(BF16)
    normed_all[pl.ds(32, rows), :] = normed[...]
    total = rows + 64
    seg, valid = frame_info(ends, real, where[0] - 32, total, length)
    seg_all[...] = seg
    own = normed_all[...]
    pre_value = jnp.dot(own, w2[0], preferred_element_type=F32)
    pre_gate = jnp.dot(own, w2[1], preferred_element_type=F32)
    value[...] = pre_value[32 : 32 + rows]
    gate[...] = pre_gate[32 : 32 + rows]
    glu[...] = (wide(valid, hidden) * pre_value * jax.nn.sigmoid(pre_gate)).astype(BF16).astype(F32)
    block = 32
    for start in range(0, rows + 32, block):
        seg_own = seg_all[pl.ds(start + 16, block), :]
        sums = taps(glu, seg_all, seg_own, kernel, lambda k: k + 1, start, block, hidden)
        for g, total_sum in enumerate(sums):
            lanes = pl.ds(g * 128, 128)
            out = total_sum + dw_bias[:, lanes]
            conv[pl.ds(start, block), lanes] = out
            act_all[pl.ds(start, block), lanes] = out * jax.nn.sigmoid(out)
    act = act_all[pl.ds(16, rows), :].astype(BF16)
    half = hidden // 2
    first = where[2] == 0
    low, high = act[:, :half], act[:, half:]
    act_keep[...] = jnp.where(first, low, high)
    act_send[...] = jnp.where(first, high, low)
    mixed[...] = dot_cols(act, w_out[...]).astype(BF16)


def backward_kernel(
    length, where, ends, real, cot, prior, following, w2, kernel, w_out, value, gate, conv,
    keep, send, back, masked, grad, seg_all,
):
    rows, hidden = cot.shape[0], w_out.shape[1]
    total = rows + 32
    seg, valid = frame_info(ends, real, where[0] - 16, total, length)
    seg_all[...] = seg
    features = cot.shape[1]
    for part, at in ((prior[pl.ds(32, 16), :], 0), (cot[...], 16), (following[pl.ds(32, 16), :], 16 + rows)):
        size = part.shape[0]
        masked[pl.ds(at, size), :] = (wide(valid[at : at + size], features) * part.astype(F32)).astype(BF16)
    grad_act = jnp.dot(masked[...], w_out[...], preferred_element_type=F32)
    out = conv[...]
    s = jax.nn.sigmoid(out)
    grad[...] = (grad_act * s * (1.0 + out * (1.0 - s))).astype(BF16).astype(F32)
    block = 32
    first = where[2] == 0
    for start in range(0, rows, block):
        seg_own = seg_all[pl.ds(start + 16, block), :]
        sums = taps(grad, seg_all, seg_own, kernel, lambda k: 31 - k, start, block, hidden)
        mask = valid[start + 16 : start + 16 + block]
        here = pl.ds(start, block)
        for g, total_sum in enumerate(sums):
            lanes = pl.ds(g * 128, 128)
            s1 = jax.nn.sigmoid(gate[here, lanes])
            grad_value = mask * total_sum * s1
            grad_gate = grad_value * value[here, lanes] * (1.0 - s1)
            grad_value, grad_gate = grad_value.astype(BF16), grad_gate.astype(BF16)
            keep[here, lanes] = jnp.where(first, grad_value, grad_gate)
            send[here, lanes] = jnp.where(first, grad_gate, grad_value)
    mine = where[2]
    back[...] = (
        dot_cols(keep[...], w2[mine]) + dot_cols(send[...], w2[1 - mine])
    ).astype(BF16)


def finish_kernel(length, where, ends, real, frames, cot, gain, m0, m1, g0, g1, mixed, grad):
    rows, features = frames.shape
    source = frames[...]
    _, valid = frame_info(ends, real, where[0], rows, length)
    branch = m0[...].astype(F32) + m1[...].astype(F32)
    mixed[...] = (source.astype(F32) + wide(valid, features) * branch).astype(BF16)
    xhat, inv_std = standard(source)
    e = (g0[...].astype(F32) + g1[...].astype(F32)) * gain[...]
    first = jnp.mean(e, axis=1, keepdims=True)
    second = jnp.mean(e * xhat, axis=1, keepdims=True)
    grad[...] = (cot[...].astype(F32) + inv_std * (e - first - xhat * second)).astype(BF16)


def weight_kernel(n, *refs):
    lefts, rights, out, left, right = refs[:8], refs[8:16], refs[16], refs[17], refs[18]
    for k in range(8):
        left[:, pl.ds(k * 128, 128)] = lefts[k][n]
        right[pl.ds(k * 128, 128), :] = rights[k][...]
    total = jnp.dot(left[...], right[...], preferred_element_type=F32)
    for zy in range(16):
        out[zy] = total[zy * 24 : zy * 24 + 24].astype(BF16)


def total_kernel(scale, where, parts, keep, send):
    total = parts[0].astype(F32)
    for k in range(1, 16):
        total = total + parts[k].astype(F32)
    total = total * scale
    low, high = total[:12], total[12:]
    first = where[2] == 0
    keep[...] = jnp.where(first, low, high)
    send[...] = jnp.where(first, high, low)


def index_of(z, y, x, c):
    return ((z * 2 + y) * 4 + x) * 2 + c


def places():
    return [(z, y, x, c) for z in range(8) for y in range(2) for x in range(4) for c in range(2)]


def to_core(values):
    return lax.ppermute(values, "ctx", [(i, i ^ 1) for i in range(128)])


def along_x(values, step):
    pairs = [(index_of(z, y, x, c), index_of(z, y, (x + step) % 4, c)) for z, y, x, c in places()]
    return lax.ppermute(values, "ctx", pairs)


def spread(values):
    groups = [[index_of(z, y, x, c) for z in range(8) for y in range(2)] for x in range(4) for c in range(2)]
    return lax.all_to_all(values, "ctx", 0, 0, axis_index_groups=groups, tiled=True)


def body(frames, norm_gain, norm_bias, w_glu, kernel, dw_bias, w_out, utt_ends, valid_frames, cotangent):
    rows, features = frames.shape
    hidden = w_out.shape[1]
    length = rows * 128
    me = lax.axis_index("ctx")
    core = lax.rem(me, 2)
    where = jnp.stack([me * rows, lax.rem(me // 2, 4), core]).astype(jnp.int32)
    gain, bias = norm_gain[None, :], norm_bias[None, :]
    info = (where, utt_ends, valid_frames)
    bind = functools.partial

    tail = jnp.concatenate([frames[rows - 32 :], cotangent[rows - 16 :]], axis=0)
    head = jnp.concatenate([frames[:32], cotangent[:16]], axis=0)
    prior = lax.ppermute(tail, "ctx", [(i, i + 1) for i in range(127)])
    following = lax.ppermute(head, "ctx", [(i + 1, i) for i in range(127)])

    picked = shape((2, features // 4, rows), BF16)
    normed, *turned = call(
        bind(norm_kernel, length),
        [shape((rows, features), BF16)] + [picked] * 4,
        [SM] * 3 + [VM] * 4,
        [pltpu.VMEM((features, rows), F32), pltpu.VMEM((features // 4, rows), F32)],
    )(*info, frames, cotangent, gain, bias)
    w2 = jnp.transpose(w_glu, (1, 0, 2))

    lefts = [turned[0]] + [along_x(turned[k], k) for k in range(1, 4)]
    lefts = lefts + [to_core(block) for block in lefts]

    wide_f32 = shape((rows, hidden), F32)
    half_act = shape((rows, hidden // 2), BF16)
    value, gate, conv, act_keep, act_send, mixed_own = call(
        bind(forward_kernel, length),
        [wide_f32, wide_f32, shape((rows + 32, hidden), F32), half_act, half_act, shape((rows, features), BF16)],
        [SM] * 3 + [VM] * 9,
        [
            pltpu.VMEM((rows + 64, features), BF16),
            pltpu.VMEM((rows + 64, hidden), F32),
            pltpu.VMEM((rows + 64, 128), jnp.int32),
            pltpu.VMEM((rows + 32, hidden), F32),
        ],
    )(*info, normed, prior, following, gain, bias, w2, kernel, dw_bias[None, :], w_out)
    mixed_other = lax.ppermute(mixed_own, "tp", [(0, 1), (1, 0)])
    act_other = to_core(act_send)
    acts = [act_keep] + [along_x(act_keep, k) for k in range(1, 4)]
    acts = acts + [act_other] + [along_x(act_other, k) for k in range(1, 4)]

    grad_pre = shape((rows, hidden), BF16)
    keep, send, back_own = call(
        bind(backward_kernel, length),
        [grad_pre, grad_pre, shape((rows, features), BF16)],
        [SM] * 3 + [VM] * 9,
        [
            pltpu.VMEM((rows + 32, features), BF16),
            pltpu.VMEM((rows + 32, hidden), F32),
            pltpu.VMEM((rows + 32, 128), jnp.int32),
        ],
    )(*info, cotangent, prior, following, w2, kernel, w_out, value, gate, conv)
    other = to_core(send)
    back_other = lax.ppermute(back_own, "tp", [(0, 1), (1, 0)])
    pres = [keep] + [along_x(keep, k) for k in range(1, 4)]
    pres = pres + [other] + [along_x(other, k) for k in range(1, 4)]

    scale = float(length) ** -0.5

    def weight_grad(n, rights):
        columns = rights[0].shape[1]
        partial = call(
            bind(weight_kernel, n),
            shape((16, 24, columns), BF16),
            [VM] * 16,
            [pltpu.VMEM((features // 4, 8 * rows), BF16), pltpu.VMEM((8 * rows, columns), BF16)],
        )(*lefts, *rights)
        mine, theirs = call(
            bind(total_kernel, scale),
            [shape((12, columns), F32)] * 2,
            [SM, VM],
        )(where, spread(partial))
        theirs = to_core(theirs)
        return jnp.where(core == 0, mine, theirs), jnp.where(core == 0, theirs, mine)

    grad_out = jnp.concatenate(weight_grad(1, acts), axis=1)
    grad_glu = jnp.stack(weight_grad(0, pres), axis=1)

    mixed, grad_frames = call(
        bind(finish_kernel, length),
        [shape((rows, features), BF16)] * 2,
        [SM] * 3 + [VM] * 7,
    )(*info, frames, cotangent, gain, mixed_own, mixed_other, back_own, back_other)
    return mixed, grad_frames, grad_glu, grad_out


def solution(mesh):
    in_specs = (
        P("ctx", None),
        P(),
        P(),
        P(None, None, "tp"),
        P(None, "tp"),
        P("tp"),
        P(None, "tp"),
        P(),
        P(),
        P("ctx", None),
    )
    out_specs = (P("ctx", None), P("ctx", None), P("ctx", None, "tp"), P("ctx", "tp"))
    return jax.shard_map(body, mesh=mesh, in_specs=in_specs, out_specs=out_specs, check_vma=False)
```

```python
import functools

import jax
import jax.numpy as jnp
from jax import lax
from jax.experimental import pallas as pl
from jax.experimental.pallas import tpu as pltpu
from jax.sharding import PartitionSpec as P

EPS = 1e-05
HALF = 15
F32 = jnp.float32
BF16 = jnp.bfloat16
VM = pltpu.VMEM
SM = pltpu.SMEM
ANY = pl.ANY
HBM = pltpu.HBM


def call(kernel, out_shape, in_spaces, scratch=(), mib=12, us=1, out_space=VM):
    return pl.pallas_call(
        kernel,
        out_shape=out_shape,
        in_specs=[pl.BlockSpec(memory_space=s) for s in in_spaces],
        out_specs=jax.tree.map(lambda _: pl.BlockSpec(memory_space=out_space), out_shape),
        scratch_shapes=list(scratch),
        compiler_params=pltpu.CompilerParams(vmem_limit_bytes=mib * 1024 * 1024),
        cost_estimate=pl.CostEstimate(flops=int(us * 1e9), bytes_accessed=int(us * 3e6), transcendentals=0),
    )


def fetch(sems, pairs):
    copies = [pltpu.make_async_copy(source, target, sems.at[n]) for n, (source, target) in enumerate(pairs)]
    for copy in copies:
        copy.start()
    return copies


def after(values, *others):
    return lax.optimization_barrier((values, others))[0]


def shape(dims, kind):
    return jax.ShapeDtypeStruct(dims, kind)


FIRST, X, CORE, INFO = range(4)


def frame_info(where, start, rows, length):
    count = (where.shape[0] - INFO) // 2
    ends = [where[INFO + u] for u in range(count)]
    real = [where[INFO + count + u] for u in range(count)]
    pos = start + lax.broadcasted_iota(jnp.int32, (rows, 128), 0)
    seg = jnp.zeros((rows, 128), jnp.int32)
    limit = jnp.zeros((rows, 128), jnp.int32) + real[0]
    for u in range(count):
        past = pos >= ends[u]
        seg = seg + past.astype(jnp.int32)
        limit = jnp.where(past, ends[u] + real[u + 1] if u + 1 < count else 0, limit)
    inside = (pos >= 0) & (pos < length) & (pos < limit)
    return seg, inside.astype(F32)


def wide(mask, columns):
    return jnp.concatenate([mask] * (columns // 128), axis=1)


def standard(rows):
    source = rows.astype(F32)
    centred = source - jnp.mean(source, axis=1, keepdims=True)
    variance = jnp.mean(centred * centred, axis=1, keepdims=True)
    inv_std = lax.rsqrt(variance + EPS)
    return centred * inv_std, inv_std


def dot_cols(left, right):
    return lax.dot_general(left, right, (((1,), (1,)), ((), ())), preferred_element_type=F32)


def edge_kernel(frames, cot, tail, head, sems):
    rows = frames.shape[0]
    pairs = (
        (frames.at[pl.ds(rows - 32, 32)], tail.at[pl.ds(0, 32)]),
        (cot.at[pl.ds(rows - 16, 16)], tail.at[pl.ds(32, 16)]),
        (frames.at[pl.ds(0, 32)], head.at[pl.ds(0, 32)]),
        (cot.at[pl.ds(0, 16)], head.at[pl.ds(32, 16)]),
    )
    for copy in fetch(sems, pairs):
        copy.wait()


def norm_kernel(length, where, frames, cot, gain, bias, normed, turned, tall, picked):
    xhat, _ = standard(frames[...])
    own = (xhat * gain[...][None, :] + bias[...][None, :]).astype(BF16)
    normed[...] = own
    rows, features = frames.shape
    _, valid = frame_info(where, where[FIRST], rows, length)
    masked = wide(valid, features) * cot[...].astype(F32)
    for n, values in enumerate((own.astype(F32), masked)):
        tall[...] = values.T
        for j in range(8):
            for zy in range(16):
                picked[pl.ds(zy * 12, 12), :] = tall[pl.ds(zy * 96 + j * 12, 12), :]
            turned[j, n] = picked[...].astype(BF16)


def taps(source, seg_source, seg_own, kernel, first_of, start, rows, columns):
    groups = columns // 128
    sums = [jnp.zeros((rows, 128), F32) for _ in range(groups)]
    for k in range(2 * HALF + 1):
        at = start + first_of(k)
        same = seg_source[pl.ds(at, rows), :] == seg_own
        for g in range(groups):
            lanes = pl.ds(g * 128, 128)
            piece = jnp.where(same, source[pl.ds(at, rows), lanes], 0.0)
            sums[g] = sums[g] + kernel[pl.ds(k, 1), lanes] * piece
    return sums


def forward_kernel(
    length, where, normed, prior, following, gain, bias, w2, kernel, dw_bias, w_out,
    value, gate, conv, act, mixed, normed_all, glu, seg_all, act_all, edges, sems,
):
    rows, hidden = normed.shape[0], w_out.shape[1]
    copies = fetch(sems, [(part.at[pl.ds(0, 32)], edges.at[n]) for n, part in enumerate((prior, following))])
    normed_all[pl.ds(32, rows), :] = normed[...]
    total = rows + 64
    seg, valid = frame_info(where, where[FIRST] - 32, total, length)
    seg_all[...] = seg
    for n, at in enumerate((0, rows + 32)):
        copies[n].wait()
        xhat, _ = standard(edges[n])
        normed_all[pl.ds(at, 32), :] = (xhat * gain[...][None, :] + bias[...][None, :]).astype(BF16)
    own = normed_all[...]
    pre_value = jnp.dot(own, w2[0], preferred_element_type=F32)
    pre_gate = jnp.dot(own, w2[1], preferred_element_type=F32)
    value[...] = pre_value[32 : 32 + rows]
    gate[...] = pre_gate[32 : 32 + rows]
    glu[...] = (wide(valid, hidden) * pre_value * jax.nn.sigmoid(pre_gate)).astype(BF16).astype(F32)
    block = 32
    for start in range(0, rows + 32, block):
        seg_own = seg_all[pl.ds(start + 16, block), :]
        sums = taps(glu, seg_all, seg_own, kernel, lambda k: k + 1, start, block, hidden)
        for g, total_sum in enumerate(sums):
            lanes = pl.ds(g * 128, 128)
            out = total_sum + dw_bias[pl.ds(g * 128, 128)][None, :]
            conv[pl.ds(start, block), lanes] = out
            act_all[pl.ds(start, block), lanes] = out * jax.nn.sigmoid(out)
    act[...] = act_all[pl.ds(16, rows), :].astype(BF16)
    mixed[...] = dot_cols(act[...], w_out[...]).astype(BF16)


def backward_kernel(
    length, where, cot, prior, following, w2, kernel, w_out, value, gate, conv,
    pre, back, masked, grad, seg_all, edges, sems,
):
    rows, hidden = cot.shape[0], w_out.shape[1]
    copies = fetch(sems, [(part.at[pl.ds(32, 16)], edges.at[n]) for n, part in enumerate((prior, following))])
    total = rows + 32
    seg, valid = frame_info(where, where[FIRST] - 16, total, length)
    seg_all[...] = seg
    features = cot.shape[1]
    for part, at in ((cot, 16), (edges.at[0], 0), (edges.at[1], 16 + rows)):
        if at != 16:
            copies[at > 0].wait()
        size = part.shape[0]
        masked[pl.ds(at, size), :] = (wide(valid[at : at + size], features) * part[...].astype(F32)).astype(BF16)
    grad_act = jnp.dot(masked[...], w_out[...], preferred_element_type=F32)
    out = conv[...]
    s = jax.nn.sigmoid(out)
    grad[...] = (grad_act * s * (1.0 + out * (1.0 - s))).astype(BF16).astype(F32)
    block = 32
    for start in range(0, rows, block):
        seg_own = seg_all[pl.ds(start + 16, block), :]
        sums = taps(grad, seg_all, seg_own, kernel, lambda k: 31 - k, start, block, hidden)
        mask = valid[start + 16 : start + 16 + block]
        here = pl.ds(start, block)
        for g, total_sum in enumerate(sums):
            lanes = pl.ds(g * 128, 128)
            s1 = jax.nn.sigmoid(gate[here, lanes])
            grad_value = mask * total_sum * s1
            grad_gate = grad_value * value[here, lanes] * (1.0 - s1)
            pre[here, lanes] = grad_value.astype(BF16)
            pre[here, pl.ds(hidden + g * 128, 128)] = grad_gate.astype(BF16)
    back[...] = (dot_cols(pre[:, :hidden], w2[0]) + dot_cols(pre[:, hidden:], w2[1])).astype(BF16)


def finish_kernel(
    length, where, frames, cot, gain, m0, m1, g0, g1, mixed, grad, held, sems
):
    rows, features = frames.shape
    copies = fetch(sems, [(part, held.at[n]) for n, part in enumerate((frames, m0, m1, g0, g1, cot))])
    _, valid = frame_info(where, where[FIRST], rows, length)
    for copy in copies:
        copy.wait()
    source = held[0]
    branch = held[1].astype(F32) + held[2].astype(F32)
    mixed[...] = (source.astype(F32) + wide(valid, features) * branch).astype(BF16)
    xhat, inv_std = standard(source)
    e = (held[3].astype(F32) + held[4].astype(F32)) * gain[...][None, :]
    first = jnp.mean(e, axis=1, keepdims=True)
    second = jnp.mean(e * xhat, axis=1, keepdims=True)
    grad[...] = (held[5].astype(F32) + inv_std * (e - first - xhat * second)).astype(BF16)


def weight_kernel(where, lefts, *refs):
    pres, acts, (out, left, right, act, total, cut, sems) = refs[:8], refs[8:16], refs[16:]
    x, core = where[X], where[CORE]
    pairs = []
    for k in range(8):
        source = lax.rem(x - (k % 4) + 4, 4) * 2 + (core if k < 4 else 1 - core)
        lanes = pl.ds(k * 128, 128)
        pairs.append((lefts.at[source, 0], left.at[0, :, lanes]))
        pairs.append((pres[k], right.at[lanes, :]))
        pairs.append((lefts.at[source, 1], left.at[1, :, lanes]))
        pairs.append((acts[k], act.at[lanes, :]))
    for copy in fetch(sems, pairs):
        copy.wait()
    wide_half, half = right.shape[1] // 2, act.shape[1] // 2
    at = 0
    for n, factor in enumerate((right, act)):
        size = factor.shape[1]
        total[:, pl.ds(at, size)] = jnp.dot(left[n], factor[...], preferred_element_type=F32)
        at = at + size
    for zy in range(16):
        rows = pl.ds(zy * 12, 12)
        for n in range(2):
            to = pl.ds(n * 12, 12)
            cut[zy, to, pl.ds(0, wide_half)] = total[rows, pl.ds(n * wide_half, wide_half)]
            cut[zy, to, pl.ds(wide_half, half)] = total[rows, pl.ds(2 * wide_half + n * half, half)]
    out[...] = cut[...].astype(BF16)


def total_kernel(scale, parts, value, gate, grad_out):
    total = parts[0].astype(F32)
    for k in range(1, 16):
        total = total + parts[k].astype(F32)
    total = total * scale
    split = value.shape[1]
    value[...] = total[:12, :split]
    gate[...] = total[12:, :split]
    half = grad_out.shape[1] // 2
    grad_out[:, :half] = total[:12, split:]
    grad_out[:, half:] = total[12:, split:]


def index_of(z, y, x, c):
    return ((z * 2 + y) * 4 + x) * 2 + c


def places():
    return [(z, y, x, c) for z in range(8) for y in range(2) for x in range(4) for c in range(2)]


def to_core(values):
    return lax.ppermute(values, "ctx", [(i, i ^ 1) for i in range(128)])


def along_x(values, step):
    pairs = [(index_of(z, y, x, c), index_of(z, y, (x + step) % 4, c)) for z, y, x, c in places()]
    return lax.ppermute(values, "ctx", pairs)


def blocks_of_x():
    return [[i * 8 + j for j in range(8)] for i in range(16)]


def in_hbm(values):
    return pltpu.with_memory_space_constraint(values, HBM)


def exchange(values):
    return lax.all_to_all(values, "ctx", 0, 0, axis_index_groups=blocks_of_x(), tiled=True)


def spread(values):
    groups = [[index_of(z, y, x, c) for z in range(8) for y in range(2)] for x in range(4) for c in range(2)]
    return lax.all_to_all(values, "ctx", 0, 0, axis_index_groups=groups, tiled=True)


def body(frames, gain, bias, w_glu, kernel, dw_bias, w_out, utt_ends, valid_frames, cotangent):
    rows, features = frames.shape
    hidden = w_out.shape[1]
    length = rows * 128
    me = lax.axis_index("ctx")
    where = jnp.concatenate([jnp.stack([me * rows, (me >> 1) & 3, me & 1]).astype(jnp.int32), utt_ends, valid_frames])
    bind = functools.partial
    dma = lambda count: pltpu.SemaphoreType.DMA((count,))

    edge = shape((48, features), BF16)
    tail, head = call(edge_kernel, [edge, edge], [HBM] * 2, [dma(4)], out_space=HBM)(
        in_hbm(frames), in_hbm(cotangent)
    )
    prior = lax.ppermute(tail, "ctx", [(i, i + 1) for i in range(127)])
    following = lax.ppermute(head, "ctx", [(i + 1, i) for i in range(127)])

    share = features // 8
    normed, turned = call(
        bind(norm_kernel, length),
        [shape((rows, features), BF16), shape((8, 2, share, rows), BF16)],
        [SM] + [VM] * 4,
        [pltpu.VMEM((features, rows), F32), pltpu.VMEM((share, rows), F32)],
        us=2,
    )(where, frames, cotangent, gain, bias)
    lefts = exchange(turned)
    w2 = jnp.transpose(w_glu, (1, 0, 2))

    wide_f32 = shape((rows, hidden), F32)
    value, gate, conv, act, mixed_own = call(
        bind(forward_kernel, length),
        [wide_f32, wide_f32, shape((rows + 32, hidden), F32), shape((rows, hidden), BF16), shape((rows, features), BF16)],
        [SM, VM, ANY, ANY] + [VM] * 6,
        [
            pltpu.VMEM((rows + 64, features), BF16),
            pltpu.VMEM((rows + 64, hidden), F32),
            pltpu.VMEM((rows + 64, 128), jnp.int32),
            pltpu.VMEM((rows + 32, hidden), F32),
            pltpu.VMEM((2, 32, features), BF16),
            dma(2),
        ],
        us=7,
    )(where, normed, prior, following, gain, bias, w2, kernel, dw_bias, w_out)
    mixed_other = lax.ppermute(mixed_own, "tp", [(0, 1), (1, 0)])
    acts = [act] + [along_x(act, k) for k in range(1, 4)]

    pre, back_own = call(
        bind(backward_kernel, length),
        [shape((rows, 2 * hidden), BF16), shape((rows, features), BF16)],
        [SM, VM, ANY, ANY] + [VM] * 6,
        [
            pltpu.VMEM((rows + 32, features), BF16),
            pltpu.VMEM((rows + 32, hidden), F32),
            pltpu.VMEM((rows + 32, 128), jnp.int32),
            pltpu.VMEM((2, 16, features), BF16),
            dma(2),
        ],
        us=7,
    )(where, cotangent, prior, following, w2, kernel, w_out, value, gate, conv)
    pre = after(pre, acts, lefts)
    pres = [pre] + [along_x(pre, k) for k in range(1, 4)]
    acts = acts + [to_core(block) for block in after(acts, pres[1])]
    pres = pres + [to_core(block) for block in pres]
    back_other = lax.ppermute(back_own, "tp", [(0, 1), (1, 0)])

    mixed, grad_frames = call(
        bind(finish_kernel, length),
        [shape((rows, features), BF16)] * 2,
        [SM, ANY, ANY, VM] + [ANY] * 4,
        [pltpu.VMEM((6, rows, features), BF16), dma(6)],
        us=3,
    )(where, frames, cotangent, gain, mixed_own, mixed_other, back_own, back_other)

    half = 3 * hidden // 2
    parts = spread(
        call(
            weight_kernel,
            shape((16, 24, half), BF16),
            [SM] + [HBM] * 17,
            [
                pltpu.VMEM((2, share, 8 * rows), BF16),
                pltpu.VMEM((8 * rows, 2 * hidden), BF16),
                pltpu.VMEM((8 * rows, hidden), BF16),
                pltpu.VMEM((share, 2 * half), F32),
                pltpu.VMEM((16, 24, half), F32),
                dma(32),
            ],
            mib=20,
            us=4,
        )(where, *[in_hbm(block) for block in (lefts, *after(pres, mixed), *acts)])
    )
    grad_value, grad_gate, grad_out = call(
        bind(total_kernel, float(length) ** -0.5), [shape((12, hidden), F32)] * 3, [VM]
    )(parts)
    return mixed, grad_frames, jnp.stack([grad_value, grad_gate], axis=1), grad_out


def solution(mesh):
    in_specs = (
        P("ctx", None),
        P(),
        P(),
        P(None, None, "tp"),
        P(None, "tp"),
        P("tp"),
        P(None, "tp"),
        P(),
        P(),
        P("ctx", None),
    )
    out_specs = (P("ctx", None), P("ctx", None), P("ctx", None, "tp"), P("ctx", "tp"))
    return jax.shard_map(body, mesh=mesh, in_specs=in_specs, out_specs=out_specs, check_vma=False)
```

```python
import functools

import jax
import jax.numpy as jnp
from jax import lax
from jax.experimental import pallas as pl
from jax.experimental.pallas import tpu as pltpu
from jax.sharding import PartitionSpec as P

EPS = 1e-05
HALF = 15
F32 = jnp.float32
BF16 = jnp.bfloat16
VM = pltpu.VMEM
ANY = pl.ANY
HBM = pltpu.HBM


def call(kernel, out_shape, in_spaces, scratch=(), mib=12, us=1, out_space=VM):
    return pl.pallas_call(
        kernel,
        out_shape=out_shape,
        in_specs=[pl.BlockSpec(memory_space=s) for s in in_spaces],
        out_specs=jax.tree.map(lambda _: pl.BlockSpec(memory_space=out_space), out_shape),
        scratch_shapes=list(scratch),
        compiler_params=pltpu.CompilerParams(vmem_limit_bytes=mib * 1024 * 1024),
        cost_estimate=pl.CostEstimate(flops=int(us * 1e7), bytes_accessed=int(us * 3e4), transcendentals=0),
    )


def fetch(sems, pairs):
    copies = [pltpu.make_async_copy(source, target, sems.at[n]) for n, (source, target) in enumerate(pairs)]
    for copy in copies:
        copy.start()
    return copies


def after(values, *others):
    return lax.optimization_barrier((values, others))[0]


def shape(dims, kind):
    return jax.ShapeDtypeStruct(dims, kind)


def frame_info(slots, start, rows, length):
    count = slots.shape[1]
    ends, real = ([slots[n, u] for u in range(count)] for n in range(2))
    pos = start + lax.broadcasted_iota(jnp.int32, (rows, 128), 0)
    seg = jnp.zeros((rows, 128), jnp.int32)
    limit = jnp.zeros((rows, 128), jnp.int32) + real[0]
    for u in range(count):
        past = pos >= ends[u]
        seg = seg + past.astype(jnp.int32)
        limit = jnp.where(past, ends[u] + real[u + 1] if u + 1 < count else 0, limit)
    inside = (pos >= 0) & (pos < length) & (pos < limit)
    return seg, inside.astype(F32)


def wide(mask, columns):
    return jnp.concatenate([mask] * (columns // 128), axis=1)


def standard(rows):
    source = rows.astype(F32)
    centred = source - jnp.mean(source, axis=1, keepdims=True)
    variance = jnp.mean(centred * centred, axis=1, keepdims=True)
    inv_std = lax.rsqrt(variance + EPS)
    return centred * inv_std, inv_std


def dot_cols(left, right):
    return lax.dot_general(left, right, (((1,), (1,)), ((), ())), preferred_element_type=F32)


def edge_kernel(frames, cot, tail, head, sems):
    rows = frames.shape[0]
    pairs = (
        (frames.at[pl.ds(rows - 32, 32)], tail.at[pl.ds(0, 32)]),
        (cot.at[pl.ds(rows - 16, 16)], tail.at[pl.ds(32, 16)]),
        (frames.at[pl.ds(0, 32)], head.at[pl.ds(0, 32)]),
        (cot.at[pl.ds(0, 16)], head.at[pl.ds(32, 16)]),
    )
    for copy in fetch(sems, pairs):
        copy.wait()


def norm_kernel(
    length, ends, real, frames, cot, gain, bias, normed, t0, t1, t2, t3, tall, picked, slots, held, shift, sems
):
    copies = fetch(sems, [
        (frames, held.at[0]), (gain, shift.at[0]), (bias, shift.at[1]), (cot, held.at[1]),
        (ends, slots.at[0]), (real, slots.at[1]),
    ])
    for copy in copies[:3]:
        copy.wait()
    xhat, _ = standard(held[0])
    own = (xhat * shift[pl.ds(0, 1), :] + shift[pl.ds(1, 1), :]).astype(BF16)
    normed[...] = own
    rows, features = own.shape
    for copy in copies[3:]:
        copy.wait()
    me = lax.axis_index("ctx")
    _, valid = frame_info(slots, me * rows, rows, length)
    masked = wide(valid, features) * held[1].astype(F32)
    x = (me >> 1) & 3
    for n, values in enumerate((own.astype(F32), masked)):
        tall[...] = values.T
        for k, out in enumerate((t0, t1, t2, t3)):
            first = ((x + k) & 3) * 24
            for core in range(2):
                for zy in range(16):
                    picked[pl.ds(zy * 12, 12), :] = tall[pl.ds(zy * 96 + core * 12 + first, 12), :]
                out[core, n] = picked[...].astype(BF16)


def taps(source, seg_source, seg_own, kernel, first_of, start, rows, columns):
    groups = columns // 128
    sums = [jnp.zeros((rows, 128), F32) for _ in range(groups)]
    for k in range(2 * HALF + 1):
        at = start + first_of(k)
        same = seg_source[pl.ds(at, rows), :] == seg_own
        for g in range(groups):
            lanes = pl.ds(g * 128, 128)
            piece = jnp.where(same, source[pl.ds(at, rows), lanes], 0.0)
            sums[g] = sums[g] + kernel[pl.ds(k, 1), lanes] * piece
    return sums


def forward_kernel(
    length, ends, real, normed, prior, following, gain, bias, w2, kernel, dw_bias, w_out,
    value, gate, conv, act, mixed, normed_all, glu, seg_all, act_all, slots, edges, sems,
):
    rows, hidden = normed.shape[0], w_out.shape[1]
    copies = fetch(sems, [
        (prior.at[pl.ds(0, 32)], edges.at[0]), (following.at[pl.ds(0, 32)], edges.at[1]),
        (ends, slots.at[0]), (real, slots.at[1]),
    ])
    for copy in copies[2:]:
        copy.wait()
    normed_all[pl.ds(32, rows), :] = normed[...]
    total = rows + 64
    seg, valid = frame_info(slots, lax.axis_index("ctx") * rows - 32, total, length)
    seg_all[...] = seg
    for n, at in enumerate((0, rows + 32)):
        copies[n].wait()
        xhat, _ = standard(edges[n])
        normed_all[pl.ds(at, 32), :] = (xhat * gain[...][None, :] + bias[...][None, :]).astype(BF16)
    own = normed_all[...]
    pre_value = jnp.dot(own, w2[0], preferred_element_type=F32)
    pre_gate = jnp.dot(own, w2[1], preferred_element_type=F32)
    value[...] = pre_value[32 : 32 + rows]
    gate[...] = pre_gate[32 : 32 + rows]
    glu[...] = (wide(valid, hidden) * pre_value * jax.nn.sigmoid(pre_gate)).astype(BF16).astype(F32)
    block = 32
    for start in range(0, rows + 32, block):
        seg_own = seg_all[pl.ds(start + 16, block), :]
        sums = taps(glu, seg_all, seg_own, kernel, lambda k: k + 1, start, block, hidden)
        for g, total_sum in enumerate(sums):
            lanes = pl.ds(g * 128, 128)
            out = total_sum + dw_bias[pl.ds(g * 128, 128)][None, :]
            conv[pl.ds(start, block), lanes] = out
            act_all[pl.ds(start, block), lanes] = out * jax.nn.sigmoid(out)
    act[...] = act_all[pl.ds(16, rows), :].astype(BF16)
    mixed[...] = dot_cols(act[...], w_out[...]).astype(BF16)


def backward_kernel(
    length, ends, real, cot, prior, following, w2, kernel, w_out, value, gate, conv,
    pre, back, masked, grad, seg_all, slots, edges, sems,
):
    rows, hidden = cot.shape[0], w_out.shape[1]
    copies = fetch(sems, [
        (prior.at[pl.ds(32, 16)], edges.at[0]), (following.at[pl.ds(32, 16)], edges.at[1]),
        (ends, slots.at[0]), (real, slots.at[1]),
    ])
    for copy in copies[2:]:
        copy.wait()
    total = rows + 32
    seg, valid = frame_info(slots, lax.axis_index("ctx") * rows - 16, total, length)
    seg_all[...] = seg
    features = cot.shape[1]
    for part, at in ((cot, 16), (edges.at[0], 0), (edges.at[1], 16 + rows)):
        if at != 16:
            copies[at > 0].wait()
        size = part.shape[0]
        masked[pl.ds(at, size), :] = (wide(valid[at : at + size], features) * part[...].astype(F32)).astype(BF16)
    grad_act = jnp.dot(masked[...], w_out[...], preferred_element_type=F32)
    out = conv[...]
    s = jax.nn.sigmoid(out)
    grad[...] = (grad_act * s * (1.0 + out * (1.0 - s))).astype(BF16).astype(F32)
    block = 32
    for start in range(0, rows, block):
        seg_own = seg_all[pl.ds(start + 16, block), :]
        sums = taps(grad, seg_all, seg_own, kernel, lambda k: 31 - k, start, block, hidden)
        mask = valid[start + 16 : start + 16 + block]
        here = pl.ds(start, block)
        for g, total_sum in enumerate(sums):
            lanes = pl.ds(g * 128, 128)
            s1 = jax.nn.sigmoid(gate[here, lanes])
            grad_value = mask * total_sum * s1
            grad_gate = grad_value * value[here, lanes] * (1.0 - s1)
            pre[here, lanes] = grad_value.astype(BF16)
            pre[here, pl.ds(hidden + g * 128, 128)] = grad_gate.astype(BF16)
    back[...] = (dot_cols(pre[:, :hidden], w2[0]) + dot_cols(pre[:, hidden:], w2[1])).astype(BF16)


def finish_kernel(
    length, ends, real, frames, cot, gain, m0, m1, g0, g1, mixed, grad, slots, held, sems
):
    rows, features = frames.shape
    pairs = [(part, held.at[n]) for n, part in enumerate((frames, m0, m1, g0, g1, cot))]
    for copy in fetch(sems, pairs + [(ends, slots.at[0]), (real, slots.at[1])]):
        copy.wait()
    _, valid = frame_info(slots, lax.axis_index("ctx") * rows, rows, length)
    source = held[0]
    branch = held[1].astype(F32) + held[2].astype(F32)
    mixed[...] = (source.astype(F32) + wide(valid, features) * branch).astype(BF16)
    xhat, inv_std = standard(source)
    e = (held[3].astype(F32) + held[4].astype(F32)) * gain[...][None, :]
    first = jnp.mean(e, axis=1, keepdims=True)
    second = jnp.mean(e * xhat, axis=1, keepdims=True)
    grad[...] = (held[5].astype(F32) + inv_std * (e - first - xhat * second)).astype(BF16)


def weight_kernel(n, *refs):
    lefts, rights, (out, left, right, total, cut, sems) = refs[:8], refs[8:16], refs[16:]
    core = lax.axis_index("ctx") & 1
    pairs = []
    for k in range(8):
        frames = pl.ds(k * 128, 128)
        pairs.append((lefts[k].at[core, n], left.at[:, frames]))
        pairs.append((rights[k], right.at[frames, :]))
    copies = fetch(sems, pairs)
    for step in range(4):
        for copy in copies[4 * step : 4 * step + 4]:
            copy.wait()
        frames = pl.ds(step * 256, 256)
        term = jnp.dot(left[:, frames], right[frames, :], preferred_element_type=F32)
        total[...] = term if step == 0 else total[...] + term
    half = total.shape[1] // 2
    for zy in range(16):
        rows = pl.ds(zy * 12, 12)
        cut[zy, pl.ds(0, 12), :] = total[rows, pl.ds(0, half)]
        cut[zy, pl.ds(12, 12), :] = total[rows, pl.ds(half, half)]
    out[...] = cut[...].astype(BF16)


def total_kernel(scale, parts, out):
    total = parts[0].astype(F32)
    for k in range(1, 16):
        total = total + parts[k].astype(F32)
    total = total * scale
    if len(out.shape) == 3:
        out[:, 0, :] = total[:12]
        out[:, 1, :] = total[12:]
    else:
        half = total.shape[1]
        out[:, :half] = total[:12]
        out[:, half:] = total[12:]


def index_of(z, y, x, c):
    return ((z * 2 + y) * 4 + x) * 2 + c


def places():
    return [(z, y, x, c) for z in range(8) for y in range(2) for x in range(4) for c in range(2)]


def to_core(values):
    return lax.ppermute(values, "ctx", [(i, i ^ 1) for i in range(128)])


def along_x(values, step):
    pairs = [(index_of(z, y, x, c), index_of(z, y, (x + step) % 4, c)) for z, y, x, c in places()]
    return lax.ppermute(values, "ctx", pairs)


def in_hbm(values):
    return pltpu.with_memory_space_constraint(values, HBM)


def spread(values):
    groups = [[index_of(z, y, x, c) for z in range(8) for y in range(2)] for x in range(4) for c in range(2)]
    return lax.all_to_all(values, "ctx", 0, 0, axis_index_groups=groups, tiled=True)


def body(frames, gain, bias, w_glu, kernel, dw_bias, w_out, utt_ends, valid_frames, cotangent):
    rows, features = frames.shape
    hidden = w_out.shape[1]
    length = rows * 128
    info = (in_hbm(utt_ends), in_hbm(valid_frames))
    bind = functools.partial
    dma = lambda count: pltpu.SemaphoreType.DMA((count,))
    slots = pltpu.SMEM((2, utt_ends.shape[0]), jnp.int32)

    edge = shape((48, features), BF16)
    tail, head = call(edge_kernel, [edge, edge], [HBM] * 2, [dma(4)], out_space=HBM)(
        in_hbm(frames), in_hbm(cotangent)
    )
    prior = lax.ppermute(tail, "ctx", [(i, i + 1) for i in range(127)])
    following = lax.ppermute(head, "ctx", [(i + 1, i) for i in range(127)])

    share = features // 8
    normed, *turned = call(
        bind(norm_kernel, length),
        [shape((rows, features), BF16)] + [shape((2, 2, share, rows), BF16)] * 4,
        [HBM] * 6,
        [
            pltpu.VMEM((features, rows), F32),
            pltpu.VMEM((share, rows), F32),
            slots,
            pltpu.VMEM((2, rows, features), BF16),
            pltpu.VMEM((2, features), F32),
            dma(6),
        ],
        us=2,
    )(*info, *[in_hbm(array) for array in (frames, cotangent, gain, bias)])
    lefts = [turned[0]] + [along_x(turned[k], k) for k in range(1, 4)]
    w2 = jnp.transpose(w_glu, (1, 0, 2))

    wide_f32 = shape((rows, hidden), F32)
    value, gate, conv, act, mixed_own = call(
        bind(forward_kernel, length),
        [wide_f32, wide_f32, shape((rows + 32, hidden), F32), shape((rows, hidden), BF16), shape((rows, features), BF16)],
        [HBM, HBM, VM, ANY, ANY] + [VM] * 6,
        [
            pltpu.VMEM((rows + 64, features), BF16),
            pltpu.VMEM((rows + 64, hidden), F32),
            pltpu.VMEM((rows + 64, 128), jnp.int32),
            pltpu.VMEM((rows + 32, hidden), F32),
            slots,
            pltpu.VMEM((2, 32, features), BF16),
            dma(4),
        ],
        us=7,
    )(*info, normed, prior, following, gain, bias, w2, kernel, dw_bias, w_out)
    acts = [act] + [along_x(act, k) for k in range(1, 4)]

    pre, back_own = call(
        bind(backward_kernel, length),
        [shape((rows, 2 * hidden), BF16), shape((rows, features), BF16)],
        [HBM, HBM, VM, ANY, ANY] + [VM] * 6,
        [
            pltpu.VMEM((rows + 32, features), BF16),
            pltpu.VMEM((rows + 32, hidden), F32),
            pltpu.VMEM((rows + 32, 128), jnp.int32),
            slots,
            pltpu.VMEM((2, 16, features), BF16),
            dma(4),
        ],
        us=700,
    )(*info, cotangent, prior, following, w2, kernel, w_out, value, gate, conv)
    lefts, acts = after((lefts, acts), pre)
    lefts = lefts + [to_core(block) for block in lefts]
    acts = acts + [to_core(block) for block in acts]
    pre = after(pre, acts, lefts)
    pres = [pre] + [along_x(pre, k) for k in range(1, 4)]

    mixed_own, back_own = after((mixed_own, back_own), pres[1])
    mixed_other = lax.ppermute(mixed_own, "tp", [(0, 1), (1, 0)])
    back_other = lax.ppermute(back_own, "tp", [(0, 1), (1, 0)])

    def partial_of(n, rights, us):
        columns = rights[0].shape[1]
        return call(
            bind(weight_kernel, n),
            shape((16, 24, columns // 2), BF16),
            [HBM] * 16,
            [
                pltpu.VMEM((share, 8 * rows), BF16),
                pltpu.VMEM((8 * rows, columns), BF16),
                pltpu.VMEM((share, columns), F32),
                pltpu.VMEM((16, 24, columns // 2), F32),
                dma(16),
            ],
            mib=16,
            us=us,
        )(*[in_hbm(block) for block in (*lefts, *rights)])

    scale = float(length) ** -0.5
    out_partial = partial_of(1, acts, 2)
    out_parts = spread(out_partial)
    pres = pres + [to_core(block) for block in pres]
    glu_parts = spread(partial_of(0, after(pres, mixed_other, back_other), 3))

    mixed, grad_frames = call(
        bind(finish_kernel, length),
        [shape((rows, features), BF16)] * 2,
        [HBM, HBM, ANY, ANY, VM] + [ANY] * 4,
        [slots, pltpu.VMEM((6, rows, features), BF16), dma(8)],
        us=3,
    )(*info, frames, cotangent, gain, mixed_own, mixed_other, back_own, back_other)
    grad_out = call(bind(total_kernel, scale), shape((12, hidden), F32), [VM])(out_parts)
    grad_glu = call(bind(total_kernel, scale), shape((12, 2, hidden), F32), [VM])(glu_parts)
    return mixed, grad_frames, grad_glu, grad_out


def solution(mesh):
    in_specs = (
        P("ctx", None),
        P(),
        P(),
        P(None, None, "tp"),
        P(None, "tp"),
        P("tp"),
        P(None, "tp"),
        P(),
        P(),
        P("ctx", None),
    )
    out_specs = (P("ctx", None), P("ctx", None), P("ctx", None, "tp"), P("ctx", "tp"))
    return jax.shard_map(body, mesh=mesh, in_specs=in_specs, out_specs=out_specs, check_vma=False)
```

```python
import functools

import jax
import jax.numpy as jnp
from jax import lax
from jax.experimental import pallas as pl
from jax.experimental.pallas import tpu as pltpu
from jax.sharding import PartitionSpec as P

EPS = 1e-05
HALF = 15
F32 = jnp.float32
BF16 = jnp.bfloat16
VM = pltpu.VMEM
ANY = pl.ANY
HBM = pltpu.HBM


def call(kernel, out_shape, in_spaces, scratch=(), mib=12, us=1, out_space=VM):
    return pl.pallas_call(
        kernel,
        out_shape=out_shape,
        in_specs=[pl.BlockSpec(memory_space=s) for s in in_spaces],
        out_specs=jax.tree.map(lambda _: pl.BlockSpec(memory_space=out_space), out_shape),
        scratch_shapes=list(scratch),
        compiler_params=pltpu.CompilerParams(vmem_limit_bytes=mib * 1024 * 1024),
        cost_estimate=pl.CostEstimate(flops=int(us * 1e7), bytes_accessed=int(us * 3e4), transcendentals=0),
    )


def fetch(sems, pairs):
    copies = [pltpu.make_async_copy(source, target, sems.at[n]) for n, (source, target) in enumerate(pairs)]
    for copy in copies:
        copy.start()
    return copies


def after(values, *others):
    return lax.optimization_barrier((values, others))[0]


def shape(dims, kind):
    return jax.ShapeDtypeStruct(dims, kind)


def frame_info(slots, start, rows, length):
    count = slots.shape[1]
    ends, real = ([slots[n, u] for u in range(count)] for n in range(2))
    pos = start + lax.broadcasted_iota(jnp.int32, (rows, 128), 0)
    seg = jnp.zeros((rows, 128), jnp.int32)
    limit = jnp.zeros((rows, 128), jnp.int32) + real[0]
    for u in range(count):
        past = pos >= ends[u]
        seg = seg + past.astype(jnp.int32)
        limit = jnp.where(past, ends[u] + real[u + 1] if u + 1 < count else 0, limit)
    inside = (pos >= 0) & (pos < length) & (pos < limit)
    return seg, inside.astype(F32)


def wide(mask, columns):
    return jnp.concatenate([mask] * (columns // 128), axis=1)


def standard(rows):
    source = rows.astype(F32)
    centred = source - jnp.mean(source, axis=1, keepdims=True)
    variance = jnp.mean(centred * centred, axis=1, keepdims=True)
    inv_std = lax.rsqrt(variance + EPS)
    return centred * inv_std, inv_std


def dot_cols(left, right):
    return lax.dot_general(left, right, (((1,), (1,)), ((), ())), preferred_element_type=F32)


def edge_kernel(frames, cot, tail, head, sems):
    rows = frames.shape[0]
    pairs = (
        (frames.at[pl.ds(rows - 32, 32)], tail.at[pl.ds(0, 32)]),
        (cot.at[pl.ds(rows - 16, 16)], tail.at[pl.ds(32, 16)]),
        (frames.at[pl.ds(0, 32)], head.at[pl.ds(0, 32)]),
        (cot.at[pl.ds(0, 16)], head.at[pl.ds(32, 16)]),
    )
    for copy in fetch(sems, pairs):
        copy.wait()


def norm_kernel(
    length, ends, real, frames, cot, gain, bias, normed, t0, t1, t2, t3, tall, picked, slots, held, shift, sems
):
    copies = fetch(sems, [
        (frames, held.at[0]), (gain, shift.at[0]), (bias, shift.at[1]), (cot, held.at[1]),
        (ends, slots.at[0]), (real, slots.at[1]),
    ])
    for copy in copies[:3]:
        copy.wait()
    xhat, _ = standard(held[0])
    own = (xhat * shift[pl.ds(0, 1), :] + shift[pl.ds(1, 1), :]).astype(BF16)
    normed[...] = own
    rows, features = own.shape
    for copy in copies[3:]:
        copy.wait()
    me = lax.axis_index("ctx")
    _, valid = frame_info(slots, me * rows, rows, length)
    masked = wide(valid, features) * held[1].astype(F32)
    x = (me >> 1) & 3
    for n, values in enumerate((own.astype(F32), masked)):
        tall[...] = values.T
        for k, out in enumerate((t0, t1, t2, t3)):
            first = ((x + k) & 3) * 24
            for core in range(2):
                for zy in range(16):
                    picked[pl.ds(zy * 12, 12), :] = tall[pl.ds(zy * 96 + core * 12 + first, 12), :]
                out[core, n] = picked[...].astype(BF16)


def taps(source, seg_source, seg_own, kernel, first_of, start, rows, columns):
    groups = columns // 128
    sums = [jnp.zeros((rows, 128), F32) for _ in range(groups)]
    for k in range(2 * HALF + 1):
        at = start + first_of(k)
        same = seg_source[pl.ds(at, rows), :] == seg_own
        for g in range(groups):
            lanes = pl.ds(g * 128, 128)
            piece = jnp.where(same, source[pl.ds(at, rows), lanes], 0.0)
            sums[g] = sums[g] + kernel[pl.ds(k, 1), lanes] * piece
    return sums


def forward_kernel(
    length, ends, real, normed, prior, following, gain, bias, w2, kernel, dw_bias, w_out,
    value, gate, conv, act, mixed, normed_all, glu, seg_all, act_all, slots, edges, sems,
):
    rows, hidden = normed.shape[0], w_out.shape[1]
    copies = fetch(sems, [
        (prior.at[pl.ds(0, 32)], edges.at[0]), (following.at[pl.ds(0, 32)], edges.at[1]),
        (ends, slots.at[0]), (real, slots.at[1]),
    ])
    for copy in copies[2:]:
        copy.wait()
    normed_all[pl.ds(32, rows), :] = normed[...]
    total = rows + 64
    seg, valid = frame_info(slots, lax.axis_index("ctx") * rows - 32, total, length)
    seg_all[...] = seg
    for n, at in enumerate((0, rows + 32)):
        copies[n].wait()
        xhat, _ = standard(edges[n])
        normed_all[pl.ds(at, 32), :] = (xhat * gain[...][None, :] + bias[...][None, :]).astype(BF16)
    own = normed_all[...]
    pre_value = jnp.dot(own, w2[0], preferred_element_type=F32)
    pre_gate = jnp.dot(own, w2[1], preferred_element_type=F32)
    value[...] = pre_value[32 : 32 + rows]
    gate[...] = pre_gate[32 : 32 + rows]
    glu[...] = (wide(valid, hidden) * pre_value * jax.nn.sigmoid(pre_gate)).astype(BF16).astype(F32)
    block = 32
    for start in range(0, rows + 32, block):
        seg_own = seg_all[pl.ds(start + 16, block), :]
        sums = taps(glu, seg_all, seg_own, kernel, lambda k: k + 1, start, block, hidden)
        for g, total_sum in enumerate(sums):
            lanes = pl.ds(g * 128, 128)
            out = total_sum + dw_bias[pl.ds(g * 128, 128)][None, :]
            conv[pl.ds(start, block), lanes] = out
            act_all[pl.ds(start, block), lanes] = out * jax.nn.sigmoid(out)
    act[...] = act_all[pl.ds(16, rows), :].astype(BF16)
    mixed[...] = dot_cols(act[...], w_out[...]).astype(BF16)


def backward_kernel(
    length, ends, real, cot, prior, following, w2, kernel, w_out, value, gate, conv,
    pre, back, masked, grad, seg_all, slots, edges, sems,
):
    rows, hidden = cot.shape[0], w_out.shape[1]
    copies = fetch(sems, [
        (prior.at[pl.ds(32, 16)], edges.at[0]), (following.at[pl.ds(32, 16)], edges.at[1]),
        (ends, slots.at[0]), (real, slots.at[1]),
    ])
    for copy in copies[2:]:
        copy.wait()
    total = rows + 32
    seg, valid = frame_info(slots, lax.axis_index("ctx") * rows - 16, total, length)
    seg_all[...] = seg
    features = cot.shape[1]
    for part, at in ((cot, 16), (edges.at[0], 0), (edges.at[1], 16 + rows)):
        if at != 16:
            copies[at > 0].wait()
        size = part.shape[0]
        masked[pl.ds(at, size), :] = (wide(valid[at : at + size], features) * part[...].astype(F32)).astype(BF16)
    grad_act = jnp.dot(masked[...], w_out[...], preferred_element_type=F32)
    out = conv[...]
    s = jax.nn.sigmoid(out)
    grad[...] = (grad_act * s * (1.0 + out * (1.0 - s))).astype(BF16).astype(F32)
    block = 32
    for start in range(0, rows, block):
        seg_own = seg_all[pl.ds(start + 16, block), :]
        sums = taps(grad, seg_all, seg_own, kernel, lambda k: 31 - k, start, block, hidden)
        mask = valid[start + 16 : start + 16 + block]
        here = pl.ds(start, block)
        for g, total_sum in enumerate(sums):
            lanes = pl.ds(g * 128, 128)
            s1 = jax.nn.sigmoid(gate[here, lanes])
            grad_value = mask * total_sum * s1
            grad_gate = grad_value * value[here, lanes] * (1.0 - s1)
            pre[here, lanes] = grad_value.astype(BF16)
            pre[here, pl.ds(hidden + g * 128, 128)] = grad_gate.astype(BF16)
    back[...] = (dot_cols(pre[:, :hidden], w2[0]) + dot_cols(pre[:, hidden:], w2[1])).astype(BF16)


def finish_kernel(
    length, ends, real, frames, cot, gain, m0, m1, g0, g1, mixed, grad, slots, held, sems
):
    rows, features = frames.shape
    pairs = [(part, held.at[n]) for n, part in enumerate((frames, m0, m1, g0, g1, cot))]
    for copy in fetch(sems, pairs + [(ends, slots.at[0]), (real, slots.at[1])]):
        copy.wait()
    _, valid = frame_info(slots, lax.axis_index("ctx") * rows, rows, length)
    source = held[0]
    branch = held[1].astype(F32) + held[2].astype(F32)
    mixed[...] = (source.astype(F32) + wide(valid, features) * branch).astype(BF16)
    xhat, inv_std = standard(source)
    e = (held[3].astype(F32) + held[4].astype(F32)) * gain[...][None, :]
    first = jnp.mean(e, axis=1, keepdims=True)
    second = jnp.mean(e * xhat, axis=1, keepdims=True)
    grad[...] = (held[5].astype(F32) + inv_std * (e - first - xhat * second)).astype(BF16)


def weight_kernel(n, *refs):
    lefts, rights, (out, left, right, total, cut, sems) = refs[:8], refs[8:16], refs[16:]
    core = lax.axis_index("ctx") & 1
    pairs = []
    for k in range(8):
        frames = pl.ds(k * 128, 128)
        pairs.append((lefts[k].at[core, n], left.at[:, frames]))
        pairs.append((rights[k], right.at[frames, :]))
    copies = fetch(sems, pairs)
    for step in range(4):
        for copy in copies[4 * step : 4 * step + 4]:
            copy.wait()
        frames = pl.ds(step * 256, 256)
        term = jnp.dot(left[:, frames], right[frames, :], preferred_element_type=F32)
        total[...] = term if step == 0 else total[...] + term
    half = total.shape[1] // 2
    for zy in range(16):
        rows = pl.ds(zy * 12, 12)
        cut[zy, pl.ds(0, 12), :] = total[rows, pl.ds(0, half)]
        cut[zy, pl.ds(12, 12), :] = total[rows, pl.ds(half, half)]
    out[...] = cut[...].astype(BF16)


def total_kernel(scale, parts, out):
    total = parts[0].astype(F32)
    for k in range(1, 16):
        total = total + parts[k].astype(F32)
    total = total * scale
    if len(out.shape) == 3:
        out[:, 0, :] = total[:12]
        out[:, 1, :] = total[12:]
    else:
        half = total.shape[1]
        out[:, :half] = total[:12]
        out[:, half:] = total[12:]


def index_of(z, y, x, c):
    return ((z * 2 + y) * 4 + x) * 2 + c


def places():
    return [(z, y, x, c) for z in range(8) for y in range(2) for x in range(4) for c in range(2)]


def to_core(values):
    return lax.ppermute(values, "ctx", [(i, i ^ 1) for i in range(128)])


def along_x(values, step):
    pairs = [(index_of(z, y, x, c), index_of(z, y, (x + step) % 4, c)) for z, y, x, c in places()]
    return lax.ppermute(values, "ctx", pairs)


def in_hbm(values):
    return pltpu.with_memory_space_constraint(values, HBM)


def spread(values):
    groups = [[index_of(z, y, x, c) for z in range(8) for y in range(2)] for x in range(4) for c in range(2)]
    return lax.all_to_all(values, "ctx", 0, 0, axis_index_groups=groups, tiled=True)


def body(frames, gain, bias, w_glu, kernel, dw_bias, w_out, utt_ends, valid_frames, cotangent):
    rows, features = frames.shape
    hidden = w_out.shape[1]
    length = rows * 128
    info = (in_hbm(utt_ends), in_hbm(valid_frames))
    bind = functools.partial
    dma = lambda count: pltpu.SemaphoreType.DMA((count,))
    slots = pltpu.SMEM((2, utt_ends.shape[0]), jnp.int32)

    edge = shape((48, features), BF16)
    tail, head = call(edge_kernel, [edge, edge], [HBM] * 2, [dma(4)], out_space=HBM)(
        in_hbm(frames), in_hbm(cotangent)
    )
    prior = lax.ppermute(tail, "ctx", [(i, i + 1) for i in range(127)])
    following = lax.ppermute(head, "ctx", [(i + 1, i) for i in range(127)])

    share = features // 8
    normed, *turned = call(
        bind(norm_kernel, length),
        [shape((rows, features), BF16)] + [shape((2, 2, share, rows), BF16)] * 4,
        [HBM] * 6,
        [
            pltpu.VMEM((features, rows), F32),
            pltpu.VMEM((share, rows), F32),
            slots,
            pltpu.VMEM((2, rows, features), BF16),
            pltpu.VMEM((2, features), F32),
            dma(6),
        ],
        us=2,
    )(*info, *[in_hbm(array) for array in (*after((frames, cotangent), tail, head), gain, bias)])
    lefts = [turned[0]] + [along_x(turned[k], k) for k in range(1, 4)]
    w2 = jnp.transpose(w_glu, (1, 0, 2))

    wide_f32 = shape((rows, hidden), F32)
    value, gate, conv, act, mixed_own = call(
        bind(forward_kernel, length),
        [wide_f32, wide_f32, shape((rows + 32, hidden), F32), shape((rows, hidden), BF16), shape((rows, features), BF16)],
        [HBM, HBM, VM, ANY, ANY] + [VM] * 6,
        [
            pltpu.VMEM((rows + 64, features), BF16),
            pltpu.VMEM((rows + 64, hidden), F32),
            pltpu.VMEM((rows + 64, 128), jnp.int32),
            pltpu.VMEM((rows + 32, hidden), F32),
            slots,
            pltpu.VMEM((2, 32, features), BF16),
            dma(4),
        ],
        us=7,
    )(*info, normed, prior, following, gain, bias, w2, kernel, dw_bias, w_out)
    mixed_other = lax.ppermute(mixed_own, "tp", [(0, 1), (1, 0)])
    acts = [act] + [along_x(act, k) for k in range(1, 4)]

    pre, back_own = call(
        bind(backward_kernel, length),
        [shape((rows, 2 * hidden), BF16), shape((rows, features), BF16)],
        [HBM, HBM, VM, ANY, ANY] + [VM] * 6,
        [
            pltpu.VMEM((rows + 32, features), BF16),
            pltpu.VMEM((rows + 32, hidden), F32),
            pltpu.VMEM((rows + 32, 128), jnp.int32),
            slots,
            pltpu.VMEM((2, 16, features), BF16),
            dma(4),
        ],
        us=700,
    )(*info, cotangent, prior, following, w2, kernel, w_out, value, gate, conv)
    acts = after(acts, pre)
    acts = acts + [to_core(block) for block in acts]
    pre = after(pre, acts, lefts)
    pres = [pre] + [along_x(pre, k) for k in range(1, 4)]
    back_other = lax.ppermute(back_own, "tp", [(0, 1), (1, 0)])
    lefts = after(lefts, pre)
    lefts = lefts + [to_core(block) for block in lefts]

    def partial_of(n, rights, us):
        columns = rights[0].shape[1]
        return call(
            bind(weight_kernel, n),
            shape((16, 24, columns // 2), BF16),
            [HBM] * 16,
            [
                pltpu.VMEM((share, 8 * rows), BF16),
                pltpu.VMEM((8 * rows, columns), BF16),
                pltpu.VMEM((share, columns), F32),
                pltpu.VMEM((16, 24, columns // 2), F32),
                dma(16),
            ],
            mib=16,
            us=us,
        )(*[in_hbm(block) for block in (*lefts, *rights)])

    scale = float(length) ** -0.5
    out_partial = partial_of(1, acts, 2)
    out_parts = spread(after(out_partial, mixed_other))
    pres[1:] = after(pres[1:], back_other)
    pres = pres + [to_core(block) for block in pres]
    glu_parts = spread(partial_of(0, pres, 3))

    mixed, grad_frames = call(
        bind(finish_kernel, length),
        [shape((rows, features), BF16)] * 2,
        [HBM, HBM, ANY, ANY, VM] + [ANY] * 4,
        [slots, pltpu.VMEM((6, rows, features), BF16), dma(8)],
        us=3,
    )(*info, frames, cotangent, gain, mixed_own, mixed_other, back_own, back_other)
    grad_out = call(bind(total_kernel, scale), shape((12, hidden), F32), [VM])(out_parts)
    grad_glu = call(bind(total_kernel, scale), shape((12, 2, hidden), F32), [VM])(glu_parts)
    return mixed, grad_frames, grad_glu, grad_out


def solution(mesh):
    in_specs = (
        P("ctx", None),
        P(),
        P(),
        P(None, None, "tp"),
        P(None, "tp"),
        P("tp"),
        P(None, "tp"),
        P(),
        P(),
        P("ctx", None),
    )
    out_specs = (P("ctx", None), P("ctx", None), P("ctx", None, "tp"), P("ctx", "tp"))
    return jax.shard_map(body, mesh=mesh, in_specs=in_specs, out_specs=out_specs, check_vma=False)
```

```python
import functools

import jax
import jax.numpy as jnp
from jax import lax
from jax.experimental import pallas as pl
from jax.experimental.pallas import tpu as pltpu
from jax.sharding import PartitionSpec as P

EPS = 1e-05
HALF = 15
F32 = jnp.float32
BF16 = jnp.bfloat16
VM = pltpu.VMEM
ANY = pl.ANY
HBM = pltpu.HBM


def call(kernel, out_shape, in_spaces, scratch=(), mib=12, us=1, out_space=VM):
    return pl.pallas_call(
        kernel,
        out_shape=out_shape,
        in_specs=[pl.BlockSpec(memory_space=s) for s in in_spaces],
        out_specs=jax.tree.map(lambda _: pl.BlockSpec(memory_space=out_space), out_shape),
        scratch_shapes=list(scratch),
        compiler_params=pltpu.CompilerParams(vmem_limit_bytes=mib * 1024 * 1024),
        cost_estimate=pl.CostEstimate(flops=int(us * 1e7), bytes_accessed=int(us * 3e4), transcendentals=0),
    )


def fetch(sems, pairs):
    copies = [pltpu.make_async_copy(source, target, sems.at[n]) for n, (source, target) in enumerate(pairs)]
    for copy in copies:
        copy.start()
    return copies


def after(values, *others):
    return lax.optimization_barrier((values, others))[0]


def shape(dims, kind):
    return jax.ShapeDtypeStruct(dims, kind)


def frame_info(slots, start, rows, length):
    count = slots.shape[1]
    ends, real = ([slots[n, u] for u in range(count)] for n in range(2))
    pos = start + lax.broadcasted_iota(jnp.int32, (rows, 128), 0)
    seg = jnp.zeros((rows, 128), jnp.int32)
    limit = jnp.zeros((rows, 128), jnp.int32) + real[0]
    for u in range(count):
        past = pos >= ends[u]
        seg = seg + past.astype(jnp.int32)
        limit = jnp.where(past, ends[u] + real[u + 1] if u + 1 < count else 0, limit)
    inside = (pos >= 0) & (pos < length) & (pos < limit)
    return seg, inside.astype(F32)


def wide(mask, columns):
    return jnp.concatenate([mask] * (columns // 128), axis=1)


def standard(rows):
    source = rows.astype(F32)
    centred = source - jnp.mean(source, axis=1, keepdims=True)
    variance = jnp.mean(centred * centred, axis=1, keepdims=True)
    inv_std = lax.rsqrt(variance + EPS)
    return centred * inv_std, inv_std


def dot_cols(left, right):
    return lax.dot_general(left, right, (((1,), (1,)), ((), ())), preferred_element_type=F32)


def edge_kernel(frames, cot, tail, head, sems):
    rows = frames.shape[0]
    pairs = (
        (frames.at[pl.ds(rows - 32, 32)], tail.at[pl.ds(0, 32)]),
        (cot.at[pl.ds(rows - 16, 16)], tail.at[pl.ds(32, 16)]),
        (frames.at[pl.ds(0, 32)], head.at[pl.ds(0, 32)]),
        (cot.at[pl.ds(0, 16)], head.at[pl.ds(32, 16)]),
    )
    for copy in fetch(sems, pairs):
        copy.wait()


def norm_kernel(
    length, ends, real, frames, cot, gain, bias, normed, t0, t1, t2, t3, tall, picked, slots, held, shift, sems
):
    copies = fetch(sems, [
        (frames, held.at[0]), (gain, shift.at[0]), (bias, shift.at[1]), (cot, held.at[1]),
        (ends, slots.at[0]), (real, slots.at[1]),
    ])
    for copy in copies[:3]:
        copy.wait()
    xhat, _ = standard(held[0])
    own = (xhat * shift[pl.ds(0, 1), :] + shift[pl.ds(1, 1), :]).astype(BF16)
    normed[...] = own
    rows, features = own.shape
    for copy in copies[3:]:
        copy.wait()
    me = lax.axis_index("ctx")
    _, valid = frame_info(slots, me * rows, rows, length)
    masked = wide(valid, features) * held[1].astype(F32)
    x = (me >> 1) & 3
    for n, values in enumerate((own.astype(F32), masked)):
        tall[...] = values.T
        for k, out in enumerate((t0, t1, t2, t3)):
            first = ((x + k) & 3) * 24
            for core in range(2):
                for zy in range(16):
                    picked[pl.ds(zy * 12, 12), :] = tall[pl.ds(zy * 96 + core * 12 + first, 12), :]
                out[core, n] = picked[...].astype(BF16)


def taps(source, seg_source, seg_own, kernel, first_of, start, rows, columns):
    groups = columns // 128
    sums = [jnp.zeros((rows, 128), F32) for _ in range(groups)]
    for k in range(2 * HALF + 1):
        at = start + first_of(k)
        same = seg_source[pl.ds(at, rows), :] == seg_own
        for g in range(groups):
            lanes = pl.ds(g * 128, 128)
            piece = jnp.where(same, source[pl.ds(at, rows), lanes], 0.0)
            sums[g] = sums[g] + kernel[pl.ds(k, 1), lanes] * piece
    return sums


def forward_kernel(
    length, ends, real, normed, prior, following, gain, bias, w2, kernel, dw_bias, w_out,
    value, gate, conv, act, mixed, normed_all, glu, seg_all, act_all, slots, edges, sems,
):
    rows, hidden = act.shape
    copies = fetch(sems, [
        (prior.at[pl.ds(0, 32)], edges.at[0]), (following.at[pl.ds(0, 32)], edges.at[1]),
        (ends, slots.at[0]), (real, slots.at[1]),
    ])
    for copy in copies[2:]:
        copy.wait()
    normed_all[pl.ds(32, rows), :] = normed[...]
    total = rows + 64
    seg, valid = frame_info(slots, lax.axis_index("ctx") * rows - 32, total, length)
    seg_all[...] = seg
    for n, at in enumerate((0, rows + 32)):
        copies[n].wait()
        xhat, _ = standard(edges[n])
        normed_all[pl.ds(at, 32), :] = (xhat * gain[...][None, :] + bias[...][None, :]).astype(BF16)
    own = normed_all[...]
    pre_value = jnp.dot(own, w2[0], preferred_element_type=F32)
    pre_gate = jnp.dot(own, w2[1], preferred_element_type=F32)
    value[...] = pre_value[32 : 32 + rows]
    gate[...] = pre_gate[32 : 32 + rows]
    glu[...] = (wide(valid, hidden) * pre_value * jax.nn.sigmoid(pre_gate)).astype(BF16).astype(F32)
    block = 32
    for start in range(0, rows + 32, block):
        seg_own = seg_all[pl.ds(start + 16, block), :]
        sums = taps(glu, seg_all, seg_own, kernel, lambda k: k + 1, start, block, hidden)
        for g, total_sum in enumerate(sums):
            lanes = pl.ds(g * 128, 128)
            out = total_sum + dw_bias[pl.ds(g * 128, 128)][None, :]
            conv[pl.ds(start, block), lanes] = out
            act_all[pl.ds(start, block), lanes] = out * jax.nn.sigmoid(out)
    act[...] = act_all[pl.ds(16, rows), :].astype(BF16)
    mixed[...] = dot_cols(act[...], w_out[...]).astype(BF16)


def backward_kernel(
    length, ends, real, cot, prior, following, w2, kernel, w_out, value, gate, conv,
    pre, back, masked, grad, seg_all, slots, edges, sems,
):
    rows, hidden = cot.shape[0], w_out.shape[1]
    copies = fetch(sems, [
        (prior.at[pl.ds(32, 16)], edges.at[0]), (following.at[pl.ds(32, 16)], edges.at[1]),
        (ends, slots.at[0]), (real, slots.at[1]),
    ])
    for copy in copies[2:]:
        copy.wait()
    total = rows + 32
    seg, valid = frame_info(slots, lax.axis_index("ctx") * rows - 16, total, length)
    seg_all[...] = seg
    features = cot.shape[1]
    for part, at in ((cot, 16), (edges.at[0], 0), (edges.at[1], 16 + rows)):
        if at != 16:
            copies[at > 0].wait()
        size = part.shape[0]
        masked[pl.ds(at, size), :] = (wide(valid[at : at + size], features) * part[...].astype(F32)).astype(BF16)
    grad_act = jnp.dot(masked[...], w_out[...], preferred_element_type=F32)
    out = conv[...]
    s = jax.nn.sigmoid(out)
    grad[...] = (grad_act * s * (1.0 + out * (1.0 - s))).astype(BF16).astype(F32)
    block = 32
    for start in range(0, rows, block):
        seg_own = seg_all[pl.ds(start + 16, block), :]
        sums = taps(grad, seg_all, seg_own, kernel, lambda k: 31 - k, start, block, hidden)
        mask = valid[start + 16 : start + 16 + block]
        here = pl.ds(start, block)
        for g, total_sum in enumerate(sums):
            lanes = pl.ds(g * 128, 128)
            s1 = jax.nn.sigmoid(gate[here, lanes])
            grad_value = mask * total_sum * s1
            grad_gate = grad_value * value[here, lanes] * (1.0 - s1)
            pre[here, lanes] = grad_value.astype(BF16)
            pre[here, pl.ds(hidden + g * 128, 128)] = grad_gate.astype(BF16)
    back[...] = (dot_cols(pre[:, :hidden], w2[0]) + dot_cols(pre[:, hidden:], w2[1])).astype(BF16)


def finish_kernel(
    length, ends, real, frames, cot, gain, m0, m1, g0, g1, mixed, grad, slots, held, sems
):
    rows, features = frames.shape
    pairs = [(part, held.at[n]) for n, part in enumerate((frames, m0, m1, g0, g1, cot))]
    for copy in fetch(sems, pairs + [(ends, slots.at[0]), (real, slots.at[1])]):
        copy.wait()
    _, valid = frame_info(slots, lax.axis_index("ctx") * rows, rows, length)
    source = held[0]
    branch = held[1].astype(F32) + held[2].astype(F32)
    mixed[...] = (source.astype(F32) + wide(valid, features) * branch).astype(BF16)
    xhat, inv_std = standard(source)
    e = (held[3].astype(F32) + held[4].astype(F32)) * gain[...][None, :]
    first = jnp.mean(e, axis=1, keepdims=True)
    second = jnp.mean(e * xhat, axis=1, keepdims=True)
    grad[...] = (held[5].astype(F32) + inv_std * (e - first - xhat * second)).astype(BF16)


def weight_kernel(*refs):
    lefts, acts, pres, (out, left, act, pre, total, cut, sems) = refs[:8], refs[8:16], refs[16:24], refs[24:]
    core = lax.axis_index("ctx") & 1
    pairs = []
    for n, rights, right in ((1, acts, act), (0, pres, pre)):
        for k in range(8):
            frames = pl.ds(k * 128, 128)
            pairs.append((lefts[k].at[core, n], left.at[n, :, frames]))
            pairs.append((rights[k], right.at[frames, :]))
    copies = fetch(sems, pairs)
    narrow, wide_half = act.shape[1] // 2, pre.shape[1] // 2
    for at, (n, right, first, half) in enumerate(((1, act, wide_half, narrow), (0, pre, 0, wide_half))):
        for step in range(2):
            for copy in copies[16 * at + 8 * step : 16 * at + 8 * step + 8]:
                copy.wait()
            frames = pl.ds(step * 512, 512)
            term = jnp.dot(left[n, :, frames], right[frames, :], preferred_element_type=F32)
            lanes = pl.ds(0, 2 * half)
            total[:, lanes] = term if step == 0 else total[:, lanes] + term
        for zy in range(16):
            rows = pl.ds(zy * 12, 12)
            for side in range(2):
                cut[zy, pl.ds(side * 12, 12), pl.ds(first, half)] = total[rows, pl.ds(side * half, half)]
    out[...] = cut[...].astype(BF16)


def total_kernel(scale, parts, glu, out):
    total = parts[0].astype(F32)
    for k in range(1, 16):
        total = total + parts[k].astype(F32)
    total = total * scale
    split = glu.shape[2]
    glu[:, 0, :] = total[:12, :split]
    glu[:, 1, :] = total[12:, :split]
    half = out.shape[1] // 2
    out[:, :half] = total[:12, split:]
    out[:, half:] = total[12:, split:]


def index_of(z, y, x, c):
    return ((z * 2 + y) * 4 + x) * 2 + c


def places():
    return [(z, y, x, c) for z in range(8) for y in range(2) for x in range(4) for c in range(2)]


def to_core(values):
    return lax.ppermute(values, "ctx", [(i, i ^ 1) for i in range(128)])


def along_x(values, step):
    pairs = [(index_of(z, y, x, c), index_of(z, y, (x + step) % 4, c)) for z, y, x, c in places()]
    return lax.ppermute(values, "ctx", pairs)


def in_hbm(values):
    return pltpu.with_memory_space_constraint(values, HBM)


def spread(values):
    groups = [[index_of(z, y, x, c) for z in range(8) for y in range(2)] for x in range(4) for c in range(2)]
    return lax.all_to_all(values, "ctx", 0, 0, axis_index_groups=groups, tiled=True)


def body(frames, gain, bias, w_glu, kernel, dw_bias, w_out, utt_ends, valid_frames, cotangent):
    rows, features = frames.shape
    hidden = w_out.shape[1]
    length = rows * 128
    info = (in_hbm(utt_ends), in_hbm(valid_frames))
    bind = functools.partial
    dma = lambda count: pltpu.SemaphoreType.DMA((count,))
    slots = pltpu.SMEM((2, utt_ends.shape[0]), jnp.int32)

    edge = shape((48, features), BF16)
    tail, head = call(edge_kernel, [edge, edge], [HBM] * 2, [dma(4)], out_space=HBM)(
        in_hbm(frames), in_hbm(cotangent)
    )
    prior = lax.ppermute(tail, "ctx", [(i, i + 1) for i in range(127)])
    following = lax.ppermute(head, "ctx", [(i + 1, i) for i in range(127)])

    share = features // 8
    normed, *turned = call(
        bind(norm_kernel, length),
        [shape((rows, features), BF16)] + [shape((2, 2, share, rows), BF16)] * 4,
        [HBM] * 6,
        [
            pltpu.VMEM((features, rows), F32),
            pltpu.VMEM((share, rows), F32),
            slots,
            pltpu.VMEM((2, rows, features), BF16),
            pltpu.VMEM((2, features), F32),
            dma(6),
        ],
        us=2,
    )(*info, *[in_hbm(array) for array in (*after((frames, cotangent), tail, head), gain, bias)])
    lefts = [turned[0]] + [along_x(turned[k], k) for k in range(1, 4)]
    w2 = jnp.transpose(w_glu, (1, 0, 2))

    wide_f32 = shape((rows, hidden), F32)
    value, gate, conv, act, mixed_own = call(
        bind(forward_kernel, length),
        [wide_f32, wide_f32, shape((rows + 32, hidden), F32), shape((rows, hidden), BF16), shape((rows, features), BF16)],
        [HBM, HBM, VM, ANY, ANY] + [VM] * 6,
        [
            pltpu.VMEM((rows + 64, features), BF16),
            pltpu.VMEM((rows + 64, hidden), F32),
            pltpu.VMEM((rows + 64, 128), jnp.int32),
            pltpu.VMEM((rows + 32, hidden), F32),
            slots,
            pltpu.VMEM((2, 32, features), BF16),
            dma(4),
        ],
        us=7,
    )(*info, normed, prior, following, gain, bias, w2, kernel, dw_bias, w_out)
    mixed_other = lax.ppermute(mixed_own, "tp", [(0, 1), (1, 0)])
    acts = [act] + [along_x(act, k) for k in range(1, 4)]

    pre, back_own = call(
        bind(backward_kernel, length),
        [shape((rows, 2 * hidden), BF16), shape((rows, features), BF16)],
        [HBM, HBM, VM, ANY, ANY] + [VM] * 6,
        [
            pltpu.VMEM((rows + 32, features), BF16),
            pltpu.VMEM((rows + 32, hidden), F32),
            pltpu.VMEM((rows + 32, 128), jnp.int32),
            slots,
            pltpu.VMEM((2, 16, features), BF16),
            dma(4),
        ],
        us=700,
    )(*info, cotangent, prior, following, w2, kernel, w_out, value, gate, conv)
    back_other = lax.ppermute(back_own, "tp", [(0, 1), (1, 0)])
    pre = after(pre, acts, lefts[:3])
    pres = [pre] + [along_x(pre, k) for k in range(1, 4)]
    lefts, acts = after((lefts, acts), pres[1])
    lefts = lefts + [to_core(block) for block in lefts]
    acts = acts + [to_core(block) for block in acts]
    pres = pres[:3] + [after(pres[3], mixed_other, back_other)]
    pres = pres + [to_core(block) for block in (after(pre, pres[1]), *pres[1:])]

    half = 3 * hidden // 2
    parts = spread(
        call(
            weight_kernel,
            shape((16, 24, half), BF16),
            [HBM] * 24,
            [
                pltpu.VMEM((2, share, 8 * rows), BF16),
                pltpu.VMEM((8 * rows, hidden), BF16),
                pltpu.VMEM((8 * rows, 2 * hidden), BF16),
                pltpu.VMEM((share, 2 * hidden), F32),
                pltpu.VMEM((16, 24, half), F32),
                dma(32),
            ],
            mib=18,
            us=4,
        )(*[in_hbm(block) for block in (*lefts, *acts, *pres)])
    )
    mixed, grad_frames = call(
        bind(finish_kernel, length),
        [shape((rows, features), BF16)] * 2,
        [HBM, HBM, ANY, ANY, VM] + [ANY] * 4,
        [slots, pltpu.VMEM((6, rows, features), BF16), dma(8)],
        us=3,
    )(*info, frames, cotangent, gain, mixed_own, mixed_other, back_own, back_other)
    grad_glu, grad_out = call(
        bind(total_kernel, float(length) ** -0.5),
        [shape((12, 2, hidden), F32), shape((12, hidden), F32)],
        [VM],
    )(parts)
    return mixed, grad_frames, grad_glu, grad_out


def solution(mesh):
    in_specs = (
        P("ctx", None),
        P(),
        P(),
        P(None, None, "tp"),
        P(None, "tp"),
        P("tp"),
        P(None, "tp"),
        P(),
        P(),
        P("ctx", None),
    )
    out_specs = (P("ctx", None), P("ctx", None), P("ctx", None, "tp"), P("ctx", "tp"))
    return jax.shard_map(body, mesh=mesh, in_specs=in_specs, out_specs=out_specs, check_vma=False)
```

```python
import functools

import jax
import jax.numpy as jnp
from jax import lax
from jax.experimental import pallas as pl
from jax.experimental.pallas import tpu as pltpu
from jax.sharding import PartitionSpec as P

EPS = 1e-05
HALF = 15
F32 = jnp.float32
BF16 = jnp.bfloat16
VM = pltpu.VMEM
ANY = pl.ANY
HBM = pltpu.HBM


def call(kernel, out_shape, in_spaces, scratch=(), mib=12, us=1, out_space=VM):
    return pl.pallas_call(
        kernel,
        out_shape=out_shape,
        in_specs=[pl.BlockSpec(memory_space=s) for s in in_spaces],
        out_specs=jax.tree.map(lambda _: pl.BlockSpec(memory_space=out_space), out_shape),
        scratch_shapes=list(scratch),
        compiler_params=pltpu.CompilerParams(vmem_limit_bytes=mib * 1024 * 1024),
        cost_estimate=pl.CostEstimate(flops=int(us * 1e7), bytes_accessed=int(us * 3e4), transcendentals=0),
    )


def fetch(sems, pairs):
    copies = [pltpu.make_async_copy(source, target, sems.at[n]) for n, (source, target) in enumerate(pairs)]
    for copy in copies:
        copy.start()
    return copies


def after(values, *others):
    return lax.optimization_barrier((values, others))[0]


def shape(dims, kind):
    return jax.ShapeDtypeStruct(dims, kind)


def frame_info(slots, start, rows, length):
    count = slots.shape[1]
    ends, real = ([slots[n, u] for u in range(count)] for n in range(2))
    pos = start + lax.broadcasted_iota(jnp.int32, (rows, 128), 0)
    seg = jnp.zeros((rows, 128), jnp.int32)
    limit = jnp.zeros((rows, 128), jnp.int32) + real[0]
    for u in range(count):
        past = pos >= ends[u]
        seg = seg + past.astype(jnp.int32)
        limit = jnp.where(past, ends[u] + real[u + 1] if u + 1 < count else 0, limit)
    inside = (pos >= 0) & (pos < length) & (pos < limit)
    return seg, inside.astype(F32)


def wide(mask, columns):
    return jnp.concatenate([mask] * (columns // 128), axis=1)


def standard(rows):
    source = rows.astype(F32)
    centred = source - jnp.mean(source, axis=1, keepdims=True)
    variance = jnp.mean(centred * centred, axis=1, keepdims=True)
    inv_std = lax.rsqrt(variance + EPS)
    return centred * inv_std, inv_std


def dot_cols(left, right):
    return lax.dot_general(left, right, (((1,), (1,)), ((), ())), preferred_element_type=F32)


def edge_kernel(frames, cot, tail, head, sems):
    rows = frames.shape[0]
    pairs = (
        (frames.at[pl.ds(rows - 32, 32)], tail.at[pl.ds(0, 32)]),
        (cot.at[pl.ds(rows - 16, 16)], tail.at[pl.ds(32, 16)]),
        (frames.at[pl.ds(0, 32)], head.at[pl.ds(0, 32)]),
        (cot.at[pl.ds(0, 16)], head.at[pl.ds(32, 16)]),
    )
    for copy in fetch(sems, pairs):
        copy.wait()


def norm_kernel(
    length, ends, real, frames, cot, gain, bias, normed, t0, t1, t2, t3, tall, picked, slots, held, shift, sems
):
    copies = fetch(sems, [
        (frames, held.at[0]), (gain, shift.at[0]), (bias, shift.at[1]), (cot, held.at[1]),
        (ends, slots.at[0]), (real, slots.at[1]),
    ])
    for copy in copies[:3]:
        copy.wait()
    xhat, _ = standard(held[0])
    own = (xhat * shift[pl.ds(0, 1), :] + shift[pl.ds(1, 1), :]).astype(BF16)
    normed[...] = own
    rows, features = own.shape
    for copy in copies[3:]:
        copy.wait()
    me = lax.axis_index("ctx")
    _, valid = frame_info(slots, me * rows, rows, length)
    masked = wide(valid, features) * held[1].astype(F32)
    x = (me >> 1) & 3
    for n, values in enumerate((own.astype(F32), masked)):
        tall[...] = values.T
        for k, out in enumerate((t0, t1, t2, t3)):
            first = ((x + k) & 3) * 24
            for core in range(2):
                for zy in range(16):
                    picked[pl.ds(zy * 12, 12), :] = tall[pl.ds(zy * 96 + core * 12 + first, 12), :]
                out[core, n] = picked[...].astype(BF16)


def taps(source, seg_source, seg_own, kernel, first_of, start, rows, columns):
    groups = columns // 128
    sums = [jnp.zeros((rows, 128), F32) for _ in range(groups)]
    for k in range(2 * HALF + 1):
        at = start + first_of(k)
        same = seg_source[pl.ds(at, rows), :] == seg_own
        for g in range(groups):
            lanes = pl.ds(g * 128, 128)
            piece = jnp.where(same, source[pl.ds(at, rows), lanes], 0.0)
            sums[g] = sums[g] + kernel[pl.ds(k, 1), lanes] * piece
    return sums


def forward_kernel(
    length, ends, real, normed, prior, following, gain, bias, w2, kernel, dw_bias, w_out,
    value, gate, conv, act, mixed, normed_all, glu, seg_all, act_all, slots, edges, sems,
):
    rows, hidden = act.shape
    copies = fetch(sems, [
        (prior.at[pl.ds(0, 32)], edges.at[0]), (following.at[pl.ds(0, 32)], edges.at[1]),
        (ends, slots.at[0]), (real, slots.at[1]),
    ])
    for copy in copies[2:]:
        copy.wait()
    normed_all[pl.ds(32, rows), :] = normed[...]
    total = rows + 64
    seg, valid = frame_info(slots, lax.axis_index("ctx") * rows - 32, total, length)
    seg_all[...] = seg
    for n, at in enumerate((0, rows + 32)):
        copies[n].wait()
        xhat, _ = standard(edges[n])
        normed_all[pl.ds(at, 32), :] = (xhat * gain[...][None, :] + bias[...][None, :]).astype(BF16)
    own = normed_all[...]
    pre_value = jnp.dot(own, w2[0], preferred_element_type=F32)
    pre_gate = jnp.dot(own, w2[1], preferred_element_type=F32)
    value[...] = pre_value[32 : 32 + rows]
    gate[...] = pre_gate[32 : 32 + rows]
    glu[...] = (wide(valid, hidden) * pre_value * jax.nn.sigmoid(pre_gate)).astype(BF16).astype(F32)
    block = 32
    for start in range(0, rows + 32, block):
        seg_own = seg_all[pl.ds(start + 16, block), :]
        sums = taps(glu, seg_all, seg_own, kernel, lambda k: k + 1, start, block, hidden)
        for g, total_sum in enumerate(sums):
            lanes = pl.ds(g * 128, 128)
            out = total_sum + dw_bias[pl.ds(g * 128, 128)][None, :]
            conv[pl.ds(start, block), lanes] = out
            act_all[pl.ds(start, block), lanes] = out * jax.nn.sigmoid(out)
    act[...] = act_all[pl.ds(16, rows), :].astype(BF16)
    mixed[...] = dot_cols(act[...], w_out[...]).astype(BF16)


def backward_kernel(
    length, ends, real, cot, prior, following, w2, kernel, w_out, value, gate, conv,
    pre, back, masked, grad, seg_all, slots, edges, sems,
):
    rows, hidden = cot.shape[0], w_out.shape[1]
    copies = fetch(sems, [
        (prior.at[pl.ds(32, 16)], edges.at[0]), (following.at[pl.ds(32, 16)], edges.at[1]),
        (ends, slots.at[0]), (real, slots.at[1]),
    ])
    for copy in copies[2:]:
        copy.wait()
    total = rows + 32
    seg, valid = frame_info(slots, lax.axis_index("ctx") * rows - 16, total, length)
    seg_all[...] = seg
    features = cot.shape[1]
    for part, at in ((cot, 16), (edges.at[0], 0), (edges.at[1], 16 + rows)):
        if at != 16:
            copies[at > 0].wait()
        size = part.shape[0]
        masked[pl.ds(at, size), :] = (wide(valid[at : at + size], features) * part[...].astype(F32)).astype(BF16)
    grad_act = jnp.dot(masked[...], w_out[...], preferred_element_type=F32)
    out = conv[...]
    s = jax.nn.sigmoid(out)
    grad[...] = (grad_act * s * (1.0 + out * (1.0 - s))).astype(BF16).astype(F32)
    block = 32
    for start in range(0, rows, block):
        seg_own = seg_all[pl.ds(start + 16, block), :]
        sums = taps(grad, seg_all, seg_own, kernel, lambda k: 31 - k, start, block, hidden)
        mask = valid[start + 16 : start + 16 + block]
        here = pl.ds(start, block)
        for g, total_sum in enumerate(sums):
            lanes = pl.ds(g * 128, 128)
            s1 = jax.nn.sigmoid(gate[here, lanes])
            grad_value = mask * total_sum * s1
            grad_gate = grad_value * value[here, lanes] * (1.0 - s1)
            pre[here, lanes] = grad_value.astype(BF16)
            pre[here, pl.ds(hidden + g * 128, 128)] = grad_gate.astype(BF16)
    back[...] = (dot_cols(pre[:, :hidden], w2[0]) + dot_cols(pre[:, hidden:], w2[1])).astype(BF16)


def finish_kernel(
    length, ends, real, frames, cot, gain, m0, m1, g0, g1, mixed, grad, slots, held, sems
):
    rows, features = frames.shape
    pairs = [(part, held.at[n]) for n, part in enumerate((frames, m0, m1, g0, g1, cot))]
    for copy in fetch(sems, pairs + [(ends, slots.at[0]), (real, slots.at[1])]):
        copy.wait()
    _, valid = frame_info(slots, lax.axis_index("ctx") * rows, rows, length)
    source = held[0]
    branch = held[1].astype(F32) + held[2].astype(F32)
    mixed[...] = (source.astype(F32) + wide(valid, features) * branch).astype(BF16)
    xhat, inv_std = standard(source)
    e = (held[3].astype(F32) + held[4].astype(F32)) * gain[...][None, :]
    first = jnp.mean(e, axis=1, keepdims=True)
    second = jnp.mean(e * xhat, axis=1, keepdims=True)
    grad[...] = (held[5].astype(F32) + inv_std * (e - first - xhat * second)).astype(BF16)


def weight_kernel(n, *refs):
    lefts, rights, (out, left, right, total, cut, sems) = refs[:8], refs[8:16], refs[16:]
    core = lax.axis_index("ctx") & 1
    pairs = []
    for k in range(8):
        frames = pl.ds(k * 128, 128)
        pairs.append((lefts[k].at[core, n], left.at[:, frames]))
        pairs.append((rights[k], right.at[frames, :]))
    copies = fetch(sems, pairs)
    for step in range(4):
        for copy in copies[4 * step : 4 * step + 4]:
            copy.wait()
        frames = pl.ds(step * 256, 256)
        term = jnp.dot(left[:, frames], right[frames, :], preferred_element_type=F32)
        total[...] = term if step == 0 else total[...] + term
    half = total.shape[1] // 2
    for zy in range(16):
        rows = pl.ds(zy * 12, 12)
        cut[zy, pl.ds(0, 12), :] = total[rows, pl.ds(0, half)]
        cut[zy, pl.ds(12, 12), :] = total[rows, pl.ds(half, half)]
    out[...] = cut[...].astype(BF16)


def total_kernel(scale, parts, out):
    total = parts[0].astype(F32)
    for k in range(1, 16):
        total = total + parts[k].astype(F32)
    total = total * scale
    if len(out.shape) == 3:
        out[:, 0, :] = total[:12]
        out[:, 1, :] = total[12:]
    else:
        half = total.shape[1]
        out[:, :half] = total[:12]
        out[:, half:] = total[12:]


def index_of(z, y, x, c):
    return ((z * 2 + y) * 4 + x) * 2 + c


def places():
    return [(z, y, x, c) for z in range(8) for y in range(2) for x in range(4) for c in range(2)]


def to_core(values):
    return lax.ppermute(values, "ctx", [(i, i ^ 1) for i in range(128)])


def along_x(values, step):
    pairs = [(index_of(z, y, x, c), index_of(z, y, (x + step) % 4, c)) for z, y, x, c in places()]
    return lax.ppermute(values, "ctx", pairs)


def in_hbm(values):
    return pltpu.with_memory_space_constraint(values, HBM)


def spread(values):
    groups = [[index_of(z, y, x, c) for z in range(8) for y in range(2)] for x in range(4) for c in range(2)]
    return lax.all_to_all(values, "ctx", 0, 0, axis_index_groups=groups, tiled=True)


def body(frames, gain, bias, w_glu, kernel, dw_bias, w_out, utt_ends, valid_frames, cotangent):
    rows, features = frames.shape
    hidden = w_out.shape[1]
    length = rows * 128
    info = (in_hbm(utt_ends), in_hbm(valid_frames))
    bind = functools.partial
    dma = lambda count: pltpu.SemaphoreType.DMA((count,))
    slots = pltpu.SMEM((2, utt_ends.shape[0]), jnp.int32)

    edge = shape((48, features), BF16)
    tail, head = call(edge_kernel, [edge, edge], [HBM] * 2, [dma(4)], out_space=HBM)(
        in_hbm(frames), in_hbm(cotangent)
    )
    prior = lax.ppermute(tail, "ctx", [(i, i + 1) for i in range(127)])
    following = lax.ppermute(head, "ctx", [(i + 1, i) for i in range(127)])

    share = features // 8
    normed, *turned = call(
        bind(norm_kernel, length),
        [shape((rows, features), BF16)] + [shape((2, 2, share, rows), BF16)] * 4,
        [HBM] * 6,
        [
            pltpu.VMEM((features, rows), F32),
            pltpu.VMEM((share, rows), F32),
            slots,
            pltpu.VMEM((2, rows, features), BF16),
            pltpu.VMEM((2, features), F32),
            dma(6),
        ],
        us=2,
    )(*info, *[in_hbm(array) for array in (*after((frames, cotangent), tail, head), gain, bias)])
    lefts = [turned[0]] + [along_x(turned[k], k) for k in range(1, 4)]
    w2 = jnp.transpose(w_glu, (1, 0, 2))

    wide_f32 = shape((rows, hidden), F32)
    value, gate, conv, act, mixed_own = call(
        bind(forward_kernel, length),
        [wide_f32, wide_f32, shape((rows + 32, hidden), F32), shape((rows, hidden), BF16), shape((rows, features), BF16)],
        [HBM, HBM, VM, ANY, ANY] + [VM] * 6,
        [
            pltpu.VMEM((rows + 64, features), BF16),
            pltpu.VMEM((rows + 64, hidden), F32),
            pltpu.VMEM((rows + 64, 128), jnp.int32),
            pltpu.VMEM((rows + 32, hidden), F32),
            slots,
            pltpu.VMEM((2, 32, features), BF16),
            dma(4),
        ],
        us=7,
    )(*info, normed, prior, following, gain, bias, w2, kernel, dw_bias, w_out)
    mixed_other = lax.ppermute(mixed_own, "tp", [(0, 1), (1, 0)])
    acts = [act] + [along_x(act, k) for k in range(1, 4)]

    pre, back_own = call(
        bind(backward_kernel, length),
        [shape((rows, 2 * hidden), BF16), shape((rows, features), BF16)],
        [HBM, HBM, VM, ANY, ANY] + [VM] * 6,
        [
            pltpu.VMEM((rows + 32, features), BF16),
            pltpu.VMEM((rows + 32, hidden), F32),
            pltpu.VMEM((rows + 32, 128), jnp.int32),
            slots,
            pltpu.VMEM((2, 16, features), BF16),
            dma(4),
        ],
        us=700,
    )(*info, cotangent, prior, following, w2, kernel, w_out, value, gate, conv)
    pre = after(pre, acts, lefts)
    pres = [pre] + [along_x(pre, k) for k in range(1, 4)]
    lefts = after(lefts, pre)
    lefts = lefts + [to_core(block) for block in lefts]
    acts = acts + [to_core(block) for block in acts]
    def partial_of(n, rights, us):
        columns = rights[0].shape[1]
        return call(
            bind(weight_kernel, n),
            shape((16, 24, columns // 2), BF16),
            [HBM] * 16,
            [
                pltpu.VMEM((share, 8 * rows), BF16),
                pltpu.VMEM((8 * rows, columns), BF16),
                pltpu.VMEM((share, columns), F32),
                pltpu.VMEM((16, 24, columns // 2), F32),
                dma(16),
            ],
            mib=16,
            us=us,
        )(*[in_hbm(block) for block in (*lefts, *rights)])

    scale = float(length) ** -0.5
    out_partial = partial_of(1, acts, 2)
    out_parts = spread(out_partial)
    back_own = after(back_own, out_partial)
    back_other = lax.ppermute(back_own, "tp", [(0, 1), (1, 0)])
    pres = pres[:1] + after(pres[1:], out_partial)
    pres = pres + [to_core(block) for block in (after(pre, pres[1]), *pres[1:])]
    glu_parts = spread(after(partial_of(0, pres, 3), back_other))

    mixed, grad_frames = call(
        bind(finish_kernel, length),
        [shape((rows, features), BF16)] * 2,
        [HBM, HBM, ANY, ANY, VM] + [ANY] * 4,
        [slots, pltpu.VMEM((6, rows, features), BF16), dma(8)],
        us=3,
    )(*info, frames, cotangent, gain, mixed_own, mixed_other, back_own, back_other)
    grad_out = call(bind(total_kernel, scale), shape((12, hidden), F32), [VM])(out_parts)
    grad_glu = call(bind(total_kernel, scale), shape((12, 2, hidden), F32), [VM])(glu_parts)
    return mixed, grad_frames, grad_glu, grad_out


def solution(mesh):
    in_specs = (
        P("ctx", None),
        P(),
        P(),
        P(None, None, "tp"),
        P(None, "tp"),
        P("tp"),
        P(None, "tp"),
        P(),
        P(),
        P("ctx", None),
    )
    out_specs = (P("ctx", None), P("ctx", None), P("ctx", None, "tp"), P("ctx", "tp"))
    return jax.shard_map(body, mesh=mesh, in_specs=in_specs, out_specs=out_specs, check_vma=False)
```

```python
import functools

import jax
import jax.numpy as jnp
from jax import lax
from jax.experimental import pallas as pl
from jax.experimental.pallas import tpu as pltpu
from jax.sharding import PartitionSpec as P

EPS = 1e-05
HALF = 15
F32 = jnp.float32
BF16 = jnp.bfloat16
VM = pltpu.VMEM
ANY = pl.ANY
HBM = pltpu.HBM


def call(kernel, out_shape, in_spaces, scratch=(), mib=12, us=1, out_space=VM):
    return pl.pallas_call(
        kernel,
        out_shape=out_shape,
        in_specs=[pl.BlockSpec(memory_space=s) for s in in_spaces],
        out_specs=jax.tree.map(lambda _: pl.BlockSpec(memory_space=out_space), out_shape),
        scratch_shapes=list(scratch),
        compiler_params=pltpu.CompilerParams(vmem_limit_bytes=mib * 1024 * 1024),
        cost_estimate=pl.CostEstimate(flops=int(us * 1e7), bytes_accessed=int(us * 3e4), transcendentals=0),
    )


def fetch(sems, pairs):
    copies = [pltpu.make_async_copy(source, target, sems.at[n]) for n, (source, target) in enumerate(pairs)]
    for copy in copies:
        copy.start()
    return copies


def after(values, *others):
    return lax.optimization_barrier((values, others))[0]


def shape(dims, kind):
    return jax.ShapeDtypeStruct(dims, kind)


def frame_info(slots, start, rows, length):
    count = slots.shape[1]
    ends, real = ([slots[n, u] for u in range(count)] for n in range(2))
    pos = start + lax.broadcasted_iota(jnp.int32, (rows, 128), 0)
    seg = jnp.zeros((rows, 128), jnp.int32)
    limit = jnp.zeros((rows, 128), jnp.int32) + real[0]
    for u in range(count):
        past = pos >= ends[u]
        seg = seg + past.astype(jnp.int32)
        limit = jnp.where(past, ends[u] + real[u + 1] if u + 1 < count else 0, limit)
    inside = (pos >= 0) & (pos < length) & (pos < limit)
    return seg, inside.astype(F32)


def wide(mask, columns):
    return jnp.concatenate([mask] * (columns // 128), axis=1)


def standard(rows):
    source = rows.astype(F32)
    centred = source - jnp.mean(source, axis=1, keepdims=True)
    variance = jnp.mean(centred * centred, axis=1, keepdims=True)
    inv_std = lax.rsqrt(variance + EPS)
    return centred * inv_std, inv_std


def dot_cols(left, right):
    return lax.dot_general(left, right, (((1,), (1,)), ((), ())), preferred_element_type=F32)


def edge_kernel(frames, cot, tail, head, sems):
    rows = frames.shape[0]
    pairs = (
        (frames.at[pl.ds(rows - 32, 32)], tail.at[pl.ds(0, 32)]),
        (cot.at[pl.ds(rows - 16, 16)], tail.at[pl.ds(32, 16)]),
        (frames.at[pl.ds(0, 32)], head.at[pl.ds(0, 32)]),
        (cot.at[pl.ds(0, 16)], head.at[pl.ds(32, 16)]),
    )
    for copy in fetch(sems, pairs):
        copy.wait()


def norm_kernel(
    length, ends, real, frames, cot, gain, bias, normed, t0, t1, t2, t3, tall, picked, slots, held, shift, sems
):
    copies = fetch(sems, [
        (frames, held.at[0]), (gain, shift.at[0]), (bias, shift.at[1]), (cot, held.at[1]),
        (ends, slots.at[0]), (real, slots.at[1]),
    ])
    for copy in copies[:3]:
        copy.wait()
    xhat, _ = standard(held[0])
    own = (xhat * shift[pl.ds(0, 1), :] + shift[pl.ds(1, 1), :]).astype(BF16)
    normed[...] = own
    rows, features = own.shape
    for copy in copies[3:]:
        copy.wait()
    me = lax.axis_index("ctx")
    _, valid = frame_info(slots, me * rows, rows, length)
    masked = wide(valid, features) * held[1].astype(F32)
    x = (me >> 1) & 3
    for n, values in enumerate((own.astype(F32), masked)):
        tall[...] = values.T
        for k, out in enumerate((t0, t1, t2, t3)):
            first = ((x + k) & 3) * 24
            for core in range(2):
                for zy in range(16):
                    picked[pl.ds(zy * 12, 12), :] = tall[pl.ds(zy * 96 + core * 12 + first, 12), :]
                out[core, n] = picked[...].astype(BF16)


def taps(source, seg_source, seg_own, kernel, first_of, start, rows, columns):
    groups = columns // 128
    sums = [jnp.zeros((rows, 128), F32) for _ in range(groups)]
    for k in range(2 * HALF + 1):
        at = start + first_of(k)
        same = seg_source[pl.ds(at, rows), :] == seg_own
        for g in range(groups):
            lanes = pl.ds(g * 128, 128)
            piece = jnp.where(same, source[pl.ds(at, rows), lanes], 0.0)
            sums[g] = sums[g] + kernel[pl.ds(k, 1), lanes] * piece
    return sums


def forward_kernel(
    length, ends, real, normed, prior, following, gain, bias, w2, kernel, dw_bias, w_out,
    value, gate, conv, act, mixed, normed_all, glu, seg_all, act_all, slots, edges, sems,
):
    rows, hidden = act.shape
    copies = fetch(sems, [
        (prior.at[pl.ds(0, 32)], edges.at[0]), (following.at[pl.ds(0, 32)], edges.at[1]),
        (ends, slots.at[0]), (real, slots.at[1]),
    ])
    for copy in copies[2:]:
        copy.wait()
    normed_all[pl.ds(32, rows), :] = normed[...]
    total = rows + 64
    seg, valid = frame_info(slots, lax.axis_index("ctx") * rows - 32, total, length)
    seg_all[...] = seg
    for n, at in enumerate((0, rows + 32)):
        copies[n].wait()
        xhat, _ = standard(edges[n])
        normed_all[pl.ds(at, 32), :] = (xhat * gain[...][None, :] + bias[...][None, :]).astype(BF16)
    own = normed_all[...]
    pre_value = jnp.dot(own, w2[0], preferred_element_type=F32)
    pre_gate = jnp.dot(own, w2[1], preferred_element_type=F32)
    value[...] = pre_value[32 : 32 + rows]
    gate[...] = pre_gate[32 : 32 + rows]
    glu[...] = (wide(valid, hidden) * pre_value * jax.nn.sigmoid(pre_gate)).astype(BF16).astype(F32)
    block = 32
    for start in range(0, rows + 32, block):
        seg_own = seg_all[pl.ds(start + 16, block), :]
        sums = taps(glu, seg_all, seg_own, kernel, lambda k: k + 1, start, block, hidden)
        for g, total_sum in enumerate(sums):
            lanes = pl.ds(g * 128, 128)
            out = total_sum + dw_bias[pl.ds(g * 128, 128)][None, :]
            conv[pl.ds(start, block), lanes] = out
            act_all[pl.ds(start, block), lanes] = out * jax.nn.sigmoid(out)
    act[...] = act_all[pl.ds(16, rows), :].astype(BF16)
    mixed[...] = dot_cols(act[...], w_out[...]).astype(BF16)


def backward_kernel(
    length, ends, real, cot, prior, following, w2, kernel, w_out, value, gate, conv,
    pre, back, masked, grad, seg_all, slots, edges, sems,
):
    rows, hidden = cot.shape[0], w_out.shape[1]
    copies = fetch(sems, [
        (prior.at[pl.ds(32, 16)], edges.at[0]), (following.at[pl.ds(32, 16)], edges.at[1]),
        (ends, slots.at[0]), (real, slots.at[1]),
    ])
    for copy in copies[2:]:
        copy.wait()
    total = rows + 32
    seg, valid = frame_info(slots, lax.axis_index("ctx") * rows - 16, total, length)
    seg_all[...] = seg
    features = cot.shape[1]
    for part, at in ((cot, 16), (edges.at[0], 0), (edges.at[1], 16 + rows)):
        if at != 16:
            copies[at > 0].wait()
        size = part.shape[0]
        masked[pl.ds(at, size), :] = (wide(valid[at : at + size], features) * part[...].astype(F32)).astype(BF16)
    grad_act = jnp.dot(masked[...], w_out[...], preferred_element_type=F32)
    out = conv[...]
    s = jax.nn.sigmoid(out)
    grad[...] = (grad_act * s * (1.0 + out * (1.0 - s))).astype(BF16).astype(F32)
    block = 32
    for start in range(0, rows, block):
        seg_own = seg_all[pl.ds(start + 16, block), :]
        sums = taps(grad, seg_all, seg_own, kernel, lambda k: 31 - k, start, block, hidden)
        mask = valid[start + 16 : start + 16 + block]
        here = pl.ds(start, block)
        for g, total_sum in enumerate(sums):
            lanes = pl.ds(g * 128, 128)
            s1 = jax.nn.sigmoid(gate[here, lanes])
            grad_value = mask * total_sum * s1
            grad_gate = grad_value * value[here, lanes] * (1.0 - s1)
            pre[here, lanes] = grad_value.astype(BF16)
            pre[here, pl.ds(hidden + g * 128, 128)] = grad_gate.astype(BF16)
    back[...] = (dot_cols(pre[:, :hidden], w2[0]) + dot_cols(pre[:, hidden:], w2[1])).astype(BF16)


def finish_kernel(
    length, ends, real, frames, cot, gain, m0, m1, g0, g1, mixed, grad, slots, held, sems
):
    rows, features = frames.shape
    pairs = [(part, held.at[n]) for n, part in enumerate((frames, m0, m1, g0, g1, cot))]
    for copy in fetch(sems, pairs + [(ends, slots.at[0]), (real, slots.at[1])]):
        copy.wait()
    _, valid = frame_info(slots, lax.axis_index("ctx") * rows, rows, length)
    source = held[0]
    branch = held[1].astype(F32) + held[2].astype(F32)
    mixed[...] = (source.astype(F32) + wide(valid, features) * branch).astype(BF16)
    xhat, inv_std = standard(source)
    e = (held[3].astype(F32) + held[4].astype(F32)) * gain[...][None, :]
    first = jnp.mean(e, axis=1, keepdims=True)
    second = jnp.mean(e * xhat, axis=1, keepdims=True)
    grad[...] = (held[5].astype(F32) + inv_std * (e - first - xhat * second)).astype(BF16)


def weight_kernel(*refs):
    lefts, acts, pres, (out, left, act, pre, total, cut, sems) = refs[:8], refs[8:16], refs[16:24], refs[24:]
    core = lax.axis_index("ctx") & 1
    pairs = []
    for n, rights, right in ((1, acts, act), (0, pres, pre)):
        for k in range(8):
            frames = pl.ds(k * 128, 128)
            pairs.append((lefts[k].at[core, n], left.at[n, :, frames]))
            pairs.append((rights[k], right.at[frames, :]))
    copies = fetch(sems, pairs)
    narrow, wide_half = act.shape[1] // 2, pre.shape[1] // 2
    for at, (n, right, first, half) in enumerate(((1, act, wide_half, narrow), (0, pre, 0, wide_half))):
        for step in range(2):
            for copy in copies[16 * at + 8 * step : 16 * at + 8 * step + 8]:
                copy.wait()
            frames = pl.ds(step * 512, 512)
            term = jnp.dot(left[n, :, frames], right[frames, :], preferred_element_type=F32)
            lanes = pl.ds(0, 2 * half)
            total[:, lanes] = term if step == 0 else total[:, lanes] + term
        for zy in range(16):
            rows = pl.ds(zy * 12, 12)
            for side in range(2):
                cut[zy, pl.ds(side * 12, 12), pl.ds(first, half)] = total[rows, pl.ds(side * half, half)]
    out[...] = cut[...].astype(BF16)


def total_kernel(scale, parts, glu, out):
    total = parts[0].astype(F32)
    for k in range(1, 16):
        total = total + parts[k].astype(F32)
    total = total * scale
    split = glu.shape[2]
    glu[:, 0, :] = total[:12, :split]
    glu[:, 1, :] = total[12:, :split]
    half = out.shape[1] // 2
    out[:, :half] = total[:12, split:]
    out[:, half:] = total[12:, split:]


def index_of(z, y, x, c):
    return ((z * 2 + y) * 4 + x) * 2 + c


def places():
    return [(z, y, x, c) for z in range(8) for y in range(2) for x in range(4) for c in range(2)]


def to_core(values):
    return lax.ppermute(values, "ctx", [(i, i ^ 1) for i in range(128)])


def along_x(values, step):
    pairs = [(index_of(z, y, x, c), index_of(z, y, (x + step) % 4, c)) for z, y, x, c in places()]
    return lax.ppermute(values, "ctx", pairs)


def in_hbm(values):
    return pltpu.with_memory_space_constraint(values, HBM)


def spread(values):
    groups = [[index_of(z, y, x, c) for z in range(8) for y in range(2)] for x in range(4) for c in range(2)]
    return lax.all_to_all(values, "ctx", 0, 0, axis_index_groups=groups, tiled=True)


def body(frames, gain, bias, w_glu, kernel, dw_bias, w_out, utt_ends, valid_frames, cotangent):
    rows, features = frames.shape
    hidden = w_out.shape[1]
    length = rows * 128
    info = (in_hbm(utt_ends), in_hbm(valid_frames))
    bind = functools.partial
    dma = lambda count: pltpu.SemaphoreType.DMA((count,))
    slots = pltpu.SMEM((2, utt_ends.shape[0]), jnp.int32)

    edge = shape((48, features), BF16)
    tail, head = call(edge_kernel, [edge, edge], [HBM] * 2, [dma(4)], out_space=HBM)(
        in_hbm(frames), in_hbm(cotangent)
    )
    prior = lax.ppermute(tail, "ctx", [(i, i + 1) for i in range(127)])
    following = lax.ppermute(head, "ctx", [(i + 1, i) for i in range(127)])

    share = features // 8
    normed, *turned = call(
        bind(norm_kernel, length),
        [shape((rows, features), BF16)] + [shape((2, 2, share, rows), BF16)] * 4,
        [HBM] * 6,
        [
            pltpu.VMEM((features, rows), F32),
            pltpu.VMEM((share, rows), F32),
            slots,
            pltpu.VMEM((2, rows, features), BF16),
            pltpu.VMEM((2, features), F32),
            dma(6),
        ],
        us=2,
    )(*info, *[in_hbm(array) for array in (*after((frames, cotangent), tail, head), gain, bias)])
    lefts = [turned[0]] + [along_x(turned[k], k) for k in range(1, 4)]
    w2 = jnp.transpose(w_glu, (1, 0, 2))

    wide_f32 = shape((rows, hidden), F32)
    value, gate, conv, act, mixed_own = call(
        bind(forward_kernel, length),
        [wide_f32, wide_f32, shape((rows + 32, hidden), F32), shape((rows, hidden), BF16), shape((rows, features), BF16)],
        [HBM, HBM, VM, ANY, ANY] + [VM] * 6,
        [
            pltpu.VMEM((rows + 64, features), BF16),
            pltpu.VMEM((rows + 64, hidden), F32),
            pltpu.VMEM((rows + 64, 128), jnp.int32),
            pltpu.VMEM((rows + 32, hidden), F32),
            slots,
            pltpu.VMEM((2, 32, features), BF16),
            dma(4),
        ],
        us=7,
    )(*info, normed, prior, following, gain, bias, w2, kernel, dw_bias, w_out)
    mixed_other = lax.ppermute(mixed_own, "tp", [(0, 1), (1, 0)])
    acts = [act] + [along_x(act, k) for k in range(1, 4)]

    pre, back_own = call(
        bind(backward_kernel, length),
        [shape((rows, 2 * hidden), BF16), shape((rows, features), BF16)],
        [HBM, HBM, VM, ANY, ANY] + [VM] * 6,
        [
            pltpu.VMEM((rows + 32, features), BF16),
            pltpu.VMEM((rows + 32, hidden), F32),
            pltpu.VMEM((rows + 32, 128), jnp.int32),
            slots,
            pltpu.VMEM((2, 16, features), BF16),
            dma(4),
        ],
        us=700,
    )(*info, cotangent, prior, following, w2, kernel, w_out, value, gate, conv)
    back_other = lax.ppermute(back_own, "tp", [(0, 1), (1, 0)])
    pre = after(pre, acts, lefts[:3])
    pres = [pre] + [along_x(pre, k) for k in range(1, 4)]
    lefts, acts = after((lefts, acts), pres[1])
    lefts = lefts + [to_core(block) for block in lefts]
    acts = acts + [to_core(block) for block in acts]
    pres = pres[:3] + [after(pres[3], back_other)]
    pres = pres + [to_core(block) for block in (after(pre, pres[1]), *pres[1:])]

    half = 3 * hidden // 2
    parts = spread(
        call(
            weight_kernel,
            shape((16, 24, half), BF16),
            [HBM] * 24,
            [
                pltpu.VMEM((2, share, 8 * rows), BF16),
                pltpu.VMEM((8 * rows, hidden), BF16),
                pltpu.VMEM((8 * rows, 2 * hidden), BF16),
                pltpu.VMEM((share, 2 * hidden), F32),
                pltpu.VMEM((16, 24, half), F32),
                dma(32),
            ],
            mib=18,
            us=4,
        )(*[in_hbm(block) for block in (*lefts, *acts, *pres)])
    )
    mixed, grad_frames = call(
        bind(finish_kernel, length),
        [shape((rows, features), BF16)] * 2,
        [HBM, HBM, ANY, ANY, VM] + [ANY] * 4,
        [slots, pltpu.VMEM((6, rows, features), BF16), dma(8)],
        us=3,
    )(*info, frames, cotangent, gain, mixed_own, mixed_other, back_own, back_other)
    grad_glu, grad_out = call(
        bind(total_kernel, float(length) ** -0.5),
        [shape((12, 2, hidden), F32), shape((12, hidden), F32)],
        [VM],
    )(parts)
    return mixed, grad_frames, grad_glu, grad_out


def solution(mesh):
    in_specs = (
        P("ctx", None),
        P(),
        P(),
        P(None, None, "tp"),
        P(None, "tp"),
        P("tp"),
        P(None, "tp"),
        P(),
        P(),
        P("ctx", None),
    )
    out_specs = (P("ctx", None), P("ctx", None), P("ctx", None, "tp"), P("ctx", "tp"))
    return jax.shard_map(body, mesh=mesh, in_specs=in_specs, out_specs=out_specs, check_vma=False)
```
